512 devices in a mesh: rep: 64 (over z, y), ch: 8 (over x, core).
Axes of the slice: x: 4, y: 8, z: 8, core: 2. Of those that a mesh axis runs over, the one named last changes fastest.
Arguments:
- inner_input: bfloat16 [384, 10, 8192], P('rep', None, 'ch'), may hold values from -6 to 6
- group_input: bfloat16 [384, 10, 8, 256], P('rep', None, 'ch'), may hold values from -6 to 6
- gate_input: bfloat16 [384, 10, 8192], P('rep', None, 'ch'), may hold values from -6 to 6
- step_size: float32 [384, 10, 128], P('rep', None, 'ch'), may hold values from -6 to 6
- scan_state: bfloat16 [384, 128, 64, 128], P('rep', 'ch'), may hold values from -6 to 6
- conv_inner: bfloat16 [384, 3, 8192], P('rep', None, 'ch'), may hold values from -6 to 6
- conv_group: bfloat16 [384, 3, 8, 256], P('rep', None, 'ch'), may hold values from -6 to 6
- prefix_scan: bfloat16 [128, 128, 64, 128], P('rep', 'ch'), may hold values from -6 to 6
- prefix_inner: bfloat16 [128, 3, 8192], P('rep', None, 'ch'), may hold values from -6 to 6
- prefix_group: bfloat16 [128, 3, 8, 256], P('rep', None, 'ch'), may hold values from -6 to 6
- inner_kernel: bfloat16 [4, 8192], P(None, 'ch'), may hold values from -3 to 3
- inner_bias: bfloat16 [8192], P('ch'), may hold values from -3 to 3
- group_kernel: bfloat16 [4, 8, 256], P(None, 'ch'), may hold values from -3 to 3
- group_bias: bfloat16 [8, 256], P('ch'), may hold values from -3 to 3
- decay_rate: float32 [128], P('ch'), may hold values from 0.02 to 2
- step_bias: float32 [128], P('ch'), may hold values from -3 to 0
- skip_gain: float32 [128], P('ch'), may hold values from 0.5 to 1.5
- norm_gain: float32 [8192], P('ch'), may hold values from 0.5 to 1.5
- event_prefix: int32 [4], replicated, may hold values from 0 to 127, as said below
- slot_event: int32 [384], P('rep'), may hold values from -1 to 3, as said below
- moved_slot: int32 [64], P('rep'), may hold values from 0 to 5
Outputs:
- layer_output: bfloat16 [384, 10, 8192], P('rep', None, 'ch')
- final_scan: bfloat16 [384, 128, 64, 128], P('rep', 'ch')
- final_inner: bfloat16 [384, 3, 8192], P('rep', None, 'ch')
- final_group: bfloat16 [384, 3, 8, 256], P('rep', None, 'ch')
The draws below stay inside these ranges and needn't reach their ends.
Inputs may be any that keep to these rules, and one draw needn't show every extreme that they name: `event_prefix`: distinct rows of the cached prefixes. `slot_event`: every value from -1 to 3 occurs.
All inputs are finite; a program needn't handle non-finite values.
Results may differ from the reference program's by a relative error of at most 0.0015.
Values may be sent and summed in bfloat16 or wider, within the bound.
A program may use at most 64 MiB of HBM per device.

```python
import math
import jax
import jax.numpy as jnp
from jax import lax

H = 128
P_SIZE = 64
N = 128
G = 8
TAPS = 4
STEPS = 10
SLOTS = 6
PREF = 2
EV = 4
ROWS = 384
PREFIXES = 128
N_REP = 64


def draw_event_prefix(key, part):
    key = jax.random.fold_in(key, 11)
    key_one, key_two = jax.random.split(key)
    total = N_REP * PREF
    middle = 1 + jax.random.permutation(key_one, total - 2)[:EV - 2]
    listed = jnp.concatenate([jnp.array([0, total - 1], dtype=jnp.int32), middle.astype(jnp.int32)])
    order = jax.random.permutation(key_two, EV)
    return listed[order].astype(jnp.int32)


def draw_slot_event(key, part):
    key = jax.random.fold_in(key, 12)
    key_one, key_two = jax.random.split(key)
    slot_total = N_REP * SLOTS
    primary = jax.random.randint(key_one, (slot_total,), -2 * EV, EV)
    secondary = jax.random.randint(key_two, (slot_total,), 0, EV)
    picked = jnp.where(primary < 0, -1, jnp.minimum(primary, secondary))
    return picked.at[0].set(EV - 1).at[1].set(-1).astype(jnp.int32)


def plant(entries, stream_key, least, largest):
    index_at = [jax.random.randint(jax.random.fold_in(stream_key, axis), (), 0, length) for axis, length in enumerate(entries.shape)]
    widest = entries.shape.index(max(entries.shape))
    next_to = index_at[:widest] + [(index_at[widest] + 1) % entries.shape[widest]] + index_at[widest + 1:]
    return entries.at[tuple(index_at)].set(least).at[tuple(next_to)].set(largest)


def levels(key, extent, cuts, low, largest):
    gain = 1.0
    for dim, shards_of in cuts:
        steps = jax.random.uniform(jax.random.fold_in(jax.random.fold_in(key, 6), dim), (shards_of,), jnp.float32, low / len(cuts), largest / len(cuts))
        gain = gain * jnp.repeat(jnp.exp(steps), extent[dim] // shards_of).reshape((-1,) + (1,) * (len(extent) - 1 - dim))
    return gain


def noise(own_key, shape, width, most, cuts=(), held_as=jnp.bfloat16):
    level = levels(own_key, shape, cuts, -0.22, 0.18) if cuts else 1.0
    drawn = jax.random.normal(own_key, shape, jnp.float32) * width * level
    return jnp.minimum(jnp.maximum(drawn, -most), most).astype(held_as)


def setup_inputs(seed: int = 0) -> dict:
    splits = jax.random.split(jax.random.key(seed), 22)
    return {
        "inner_input": noise(splits[0], (ROWS, STEPS, H * P_SIZE), 1.0, 6.0, ((0, 64), (2, 8))),
        "group_input": noise(splits[1], (ROWS, STEPS, G, 2 * N), 1.0, 6.0, ((0, 64), (2, 8))),
        "gate_input": noise(splits[2], (ROWS, STEPS, H * P_SIZE), 1.0, 6.0, ((0, 64), (2, 8))),
        "step_size": noise(splits[3], (ROWS, STEPS, H), 1.0, 6.0, ((0, 64), (2, 8)), jnp.float32),
        "scan_state": noise(splits[4], (ROWS, H, P_SIZE, N), 1.0, 6.0, ((0, 64), (1, 8))),
        "conv_inner": noise(splits[5], (ROWS, TAPS - 1, H * P_SIZE), 1.0, 6.0, ((0, 64), (2, 8))),
        "conv_group": noise(splits[6], (ROWS, TAPS - 1, G, 2 * N), 1.0, 6.0, ((0, 64), (2, 8))),
        "prefix_scan": noise(splits[7], (PREFIXES, H, P_SIZE, N), 1.0, 6.0, ((0, 64), (1, 8))),
        "prefix_inner": noise(splits[8], (PREFIXES, TAPS - 1, H * P_SIZE), 1.0, 6.0, ((0, 64), (2, 8))),
        "prefix_group": noise(splits[9], (PREFIXES, TAPS - 1, G, 2 * N), 1.0, 6.0, ((0, 64), (2, 8))),
        "inner_kernel": noise(splits[10], (TAPS, H * P_SIZE), TAPS ** -0.5, 3.0, ((1, 8),)),
        "inner_bias": noise(splits[11], (H * P_SIZE,), 0.5, 3.0, ((0, 8),)),
        "group_kernel": noise(splits[12], (TAPS, G, 2 * N), TAPS ** -0.5, 3.0, ((1, 8),)),
        "group_bias": noise(splits[13], (G, 2 * N), 0.5, 3.0, ((0, 8),)),
        "decay_rate": jnp.clip(jnp.exp(math.log(2.0) - 4.6051702 * jax.random.uniform(splits[14], (H,), jnp.float32) ** levels(splits[14], (H,), ((0, 8),), -0.2, 0.2)), 0.02, 2.0),
        "step_bias": jnp.clip(-3.0 + 3.0 * jax.random.uniform(splits[15], (H,), jnp.float32) ** levels(splits[15], (H,), ((0, 8),), -0.2, 0.2), -3.0, 0.0),
        "skip_gain": jnp.clip(0.5 + 1.0 * jax.random.uniform(splits[16], (H,), jnp.float32) ** levels(splits[16], (H,), ((0, 8),), -0.2, 0.2), 0.5, 1.5),
        "norm_gain": jnp.clip(1.0 + 0.1 * jax.random.normal(splits[17], (H * P_SIZE,), jnp.float32), 0.5, 1.5),
        "event_prefix": draw_event_prefix(jax.random.fold_in(splits[21], 71), 0),
        "slot_event": draw_slot_event(jax.random.fold_in(splits[21], 71), 0),
        "moved_slot": plant(jax.random.randint(splits[20], (N_REP,), 0, SLOTS), jax.random.fold_in(splits[20], 1), 0, SLOTS - 1).astype(jnp.int32),
    }


epsilon = 1e-05

def conv_apply(tail_cache, inputs, kernel, offset):
    step_count = inputs.shape[1]
    joined = jnp.concatenate([tail_cache.astype(jnp.float32), inputs.astype(jnp.float32)], axis=1)
    summed = offset.astype(jnp.float32)
    for tap_index in range(kernel.shape[0]):
        summed = summed + kernel[tap_index].astype(jnp.float32) * joined[:, tap_index:tap_index + step_count]
    return (jax.nn.silu(summed), joined[:, step_count:])

def run_scan(start, inner_act, group_act, step_size, decay_rate, step_bias, skip_gain, state_width):
    slot_count, step_count, row_width = inner_act.shape
    head_count = step_size.shape[2]
    group_count = group_act.shape[2]
    head_size = row_width // head_count
    carried = start
    outputs = []
    for moment in range(step_count):
        step_value = jax.nn.softplus(step_size[:, moment] + step_bias)
        retain = jnp.exp(-step_value * decay_rate)
        values = inner_act[:, moment].reshape(slot_count, head_count, head_size)
        keys_in = jnp.repeat(group_act[:, moment, :, :state_width], head_count // group_count, axis=1)
        readout = jnp.repeat(group_act[:, moment, :, state_width:], head_count // group_count, axis=1)
        carried = retain[:, :, None, None] * carried + (step_value[:, :, None] * values)[:, :, :, None] * keys_in[:, :, None, :]
        result = jnp.einsum('shpn,shn->shp', carried, readout, precision=lax.Precision.HIGHEST) + skip_gain[:, None] * values
        outputs.append(result.reshape(slot_count, row_width))
    return (jnp.stack(outputs, axis=1), carried)

def reference(inner_input, group_input, gate_input, step_size, scan_state, conv_inner, conv_group, prefix_scan, prefix_inner, prefix_group, inner_kernel, inner_bias, group_kernel, group_bias, decay_rate, step_bias, skip_gain, norm_gain, event_prefix, slot_event, moved_slot):
    slot_index = jnp.arange(N_REP * SLOTS, dtype=jnp.int32)
    replica = slot_index // SLOTS
    within = slot_index % SLOTS
    moved_here = within == moved_slot[replica]
    previous = (replica + N_REP - 1) % N_REP
    source = jnp.where(moved_here, previous * SLOTS + moved_slot[previous], slot_index).astype(jnp.int32)
    prefix_hit = slot_event >= 0
    prefix_row = event_prefix[jnp.maximum(slot_event, 0)].astype(jnp.int32)

    def one_slot(slot_number):

        def select_start(cached, stored):
            return jnp.where(prefix_hit[slot_number], stored[prefix_row[slot_number]], cached[source[slot_number]])
        start_scan = select_start(scan_state, prefix_scan).astype(jnp.float32)
        start_inner = select_start(conv_inner, prefix_inner)
        start_group = select_start(conv_group, prefix_group)
        inner_act, tail_inner = conv_apply(start_inner[None], inner_input[slot_number][None], inner_kernel, inner_bias)
        group_act, tail_group = conv_apply(start_group[None], group_input[slot_number][None], group_kernel, group_bias)
        outputs, carried = run_scan(start_scan[None], inner_act, group_act, step_size[slot_number][None], decay_rate, step_bias, skip_gain, N)
        gated = outputs * jax.nn.silu(gate_input[slot_number][None].astype(jnp.float32))
        grouped = gated.reshape(gated.shape[0], gated.shape[1], G, gated.shape[2] // G)
        norm_scale = lax.rsqrt(lax.optimization_barrier(jnp.mean(grouped * grouped, axis=-1, keepdims=True)) + epsilon)
        normed = (grouped * norm_scale).reshape(gated.shape) * norm_gain
        return (normed[0].astype(jnp.bfloat16), carried[0].astype(jnp.bfloat16), tail_inner[0].astype(jnp.bfloat16), tail_group[0].astype(jnp.bfloat16))
    mapped = lax.map(one_slot, slot_index)
    return (mapped[0], mapped[1], mapped[2], mapped[3])
```

```python
import functools

import jax
import jax.numpy as jnp
from jax import lax
from jax.experimental import pallas as pl
from jax.experimental.pallas import tpu as pltpu
from jax.sharding import PartitionSpec as P

MESH = pl.DeviceIdType.MESH
BF16 = jnp.bfloat16
F32 = jnp.float32
EPSILON = 1e-05


def silu(v):
    return v / (1.0 + jnp.exp(-v))


def split2(v):
    high = v.astype(BF16)
    low = (v - high.astype(F32)).astype(BF16)
    return high, low


class Stream:
    def __init__(self, index, n, pos1, pos2, peer1, peer2, cand, red, cand2, candc, redc, candc2, conv, sems):
        self.index, self.n = index, n
        self.pos1, self.pos2 = pos1, pos2
        self.peer1, self.peer2 = peer1, peer2
        self.cand, self.red, self.cand2 = cand, red, cand2
        self.candc, self.redc, self.candc2 = candc, redc, candc2
        self.conv = conv
        self.sems = sems


def kernel(
    n, slots, pref, events, steps, heads, hsize, state,
    inner_ref, group_ref, gate_ref, dt_ref, scan_hbm, cinner_ref, cgroup_ref, pscan_hbm, pinner_ref, pgroup_ref,
    ikern_ref, ibias_ref, gkern_ref, gbias_ref, decay_ref, dbias_ref, skip_ref, gain_ref, ep_ref, se_ref, mv_ref,
    out_ref, fin_ref,
    pool, stage, cand_a, cand_b, red_a, red_b, cand2_a, cand2_b,
    pkf, pkb, candc_a, candc_b, redc_a, redc_b, candc2_a, candc2_b, conv_a, conv_b, camec, ucf,
    join, joing, xs, gs, dts, ms, us, ys, es,
    load_sem, s1, r1, s2, r2, s3, r3, s4, r4, sc1, rc1, sc2, rc2, sc3, rc3, sc4, rc4, sm, rm,
):
    rep = lax.axis_index("rep")
    total = n * n
    py = lax.rem(rep, n)
    pz = rep // n
    width = heads * hsize
    wrows = width // 128
    gw = 2 * state
    grows = gw // 128
    piece = events * hsize // n
    per_event = n // events
    base = slots + 1
    taps = ikern_ref.shape[0]
    tail = taps - 1

    def to(r):
        return {"rep": r}

    right = lax.rem(rep + 1, total)
    left = lax.rem(rep + total - 1, total)

    loads = [pltpu.make_async_copy(scan_hbm, pool.at[0:slots], load_sem.at[0])]
    for i, (cand, pos) in enumerate(((cand_a, py), (cand_b, pz))):
        loads.append(pltpu.make_async_copy(pscan_hbm.at[:, i * n + pos], cand.at[pos], load_sem.at[1 + i]))
    for copy in loads:
        copy.start()

    barrier = pltpu.get_barrier_semaphore()
    for d in range(1, n):
        pl.semaphore_signal(barrier, inc=1, device_id=to(pz * n + lax.rem(py + d, n)), device_id_type=MESH)
        pl.semaphore_signal(barrier, inc=1, device_id=to(lax.rem(pz + d, n) * n + py), device_id_type=MESH)
    pl.semaphore_signal(barrier, inc=1, device_id=to(right), device_id_type=MESH)
    pl.semaphore_signal(barrier, inc=1, device_id=to(left), device_id_type=MESH)

    pkf[...] = jnp.zeros_like(pkf)
    moved = mv_ref[0]

    def pack(slot, inner_rows, group_rows):
        for tap in range(tail):
            for j in range(wrows):
                pkf[slot, tap * wrows + j : tap * wrows + j + 1, :] = inner_rows[tap][:, j * 128 : (j + 1) * 128]
            for j in range(grows):
                r = tail * wrows + tap * grows + j
                pkf[slot, r : r + 1, :] = group_rows[tap][:, j * 128 : (j + 1) * 128]

    p_inner = [pinner_ref[tap].astype(F32) for tap in range(tail)]
    p_group = [pgroup_ref[tap].astype(F32) for tap in range(tail)]
    for q in range(pref):
        pack(q, [v[q : q + 1] for v in p_inner], [v[q : q + 1] for v in p_group])
    m_inner = cinner_ref[moved].astype(F32)
    m_group = cgroup_ref[moved].astype(F32)
    pack(pref, [m_inner[t : t + 1] for t in range(tail)], [m_group[t : t + 1] for t in range(tail)])
    pkb[...] = pkf[...].astype(BF16)

    pl.semaphore_wait(barrier, 2 * (n - 1) + 2)

    def copy_to(src, dst, send, recv, device):
        return pltpu.make_async_remote_copy(
            src_ref=src, dst_ref=dst, send_sem=send, recv_sem=recv, device_id=to(device), device_id_type=MESH
        )

    streams = (
        Stream(0, n, py, pz, lambda j: pz * n + j, lambda k: k * n + py,
               cand_a, red_a, cand2_a, candc_a, redc_a, candc2_a, conv_a, None),
        Stream(1, n, pz, py, lambda j: j * n + py, lambda k: pz * n + k,
               cand_b, red_b, cand2_b, candc_b, redc_b, candc2_b, conv_b, None),
    )

    def owner(st, e):
        rid = ep_ref[e]
        r = rid // pref
        y, z = lax.rem(r, n), r // n
        return (y, z, lax.rem(rid, pref)) if st.index == 0 else (z, y, lax.rem(rid, pref))

    def half(i):
        return slice(i * 16, (i + 1) * 16)

    def conv1_copy(st, src_pos):
        return copy_to(
            pkb.at[0:pref, half(st.index)], st.candc.at[src_pos],
            sc1.at[st.index], rc1.at[st.index, src_pos - 1], st.peer1(0),
        )

    for st in streams:
        @pl.when(st.pos1 != 0)
        def _(st=st):
            for src in range(1, n):
                @pl.when(st.pos1 == src)
                def _(src=src):
                    conv1_copy(st, src).start()

    def rs1_copy(st, d):
        j = lax.rem(st.pos1 + d, n)
        return copy_to(
            pscan_hbm.at[:, st.index * n + j], st.cand.at[st.pos1],
            s1.at[st.index, d - 1], r1.at[st.index, d - 1], st.peer1(j),
        )

    def rs1_wait(st, d):
        j = lax.rem(st.pos1 + n - d, n)
        copy_to(
            st.cand.at[j], st.cand.at[j], s1.at[st.index, d - 1], r1.at[st.index, d - 1], st.peer1(j)
        ).wait_recv()

    for d in (n // 2, *[x for k in range(n // 2 - 1, 0, -1) for x in (k, n - k)]):
        for st in streams:
            rs1_copy(st, d).start()

    loads[0].wait()
    for h in range(heads):
        got = pool[0, h]
        for s in range(1, slots):
            got = jnp.where(moved == s, pool[s, h], got)
        stage[h] = got
    move_copies = (
        copy_to(pkb.at[pref], camec, sm.at[0], rm.at[0], right),
        copy_to(stage, pool.at[slots], sm.at[1], rm.at[1], right),
    )
    for copy in move_copies:
        copy.start()

    join[...] = jnp.zeros_like(join)
    joing[...] = jnp.zeros_like(joing)
    dts[...] = jnp.zeros_like(dts)
    for t in range(steps):
        join[tail + t, 0:slots, :] = inner_ref[t].astype(F32)
        joing[tail + t, 0:slots, :] = group_ref[t].astype(F32)
        dts[t, 0:slots, :] = dt_ref[t]
    for s in range(slots):
        ucf[s, :, 0:width] = cinner_ref[s].astype(F32)
        ucf[s, :, width : width + gw] = cgroup_ref[s].astype(F32)
    step = []
    decay = []
    for t in range(steps):
        v = dts[t] + dbias_ref[...]
        v = jnp.maximum(v, 0.0) + jnp.log1p(jnp.exp(-jnp.abs(v)))
        step.append(v)
        fall = -v * decay_ref[...]
        decay.append(fall if t == 0 else decay[-1] + fall)

    def conv2_copy(st, k):
        return copy_to(
            st.redc.at[k], st.candc2.at[st.pos2],
            sc2.at[st.index, k], rc2.at[st.index, st.pos2], st.peer2(k),
        )

    def conv_two(st):
        @pl.when(st.pos1 == 0)
        def _():
            for src in range(1, n):
                conv1_copy(st, src).wait_recv()
            st.candc[0] = pkb[0:pref, half(st.index)]
            for e in range(events):
                p, _, row = owner(st, e)
                st.redc[e] = st.candc[p, row]
            for k in range(events):
                @pl.when(st.pos2 != k)
                def _(k=k):
                    conv2_copy(st, k).start()

                @pl.when(st.pos2 == k)
                def _(k=k):
                    st.candc2[k] = st.redc[k]

    def conv3_copy(st, d, e):
        k = lax.rem(st.pos2 + d, n)
        return copy_to(
            st.conv.at[e], st.conv.at[e], sc3.at[st.index, d - 1], rc3.at[st.index, e], st.peer2(k)
        )

    def conv_three(st):
        @pl.when(st.pos1 == 0)
        def _():
            for e in range(events):
                @pl.when(st.pos2 == e)
                def _(e=e):
                    for src in range(n):
                        if src != e:
                            copy_to(
                                st.candc2.at[src], st.candc2.at[src], sc2.at[st.index, 0],
                                rc2.at[st.index, src], st.peer2(src),
                            ).wait_recv()
                    _, q, _ = owner(st, e)
                    st.conv[e] = st.candc2[q]
                    for d in range(1, n):
                        conv3_copy(st, d, e).start()

    def conv4_copy(st, d):
        j = lax.rem(st.pos1 + d, n)
        return copy_to(st.conv, st.conv, sc4.at[st.index, d - 1], rc4.at[st.index], st.peer1(j))

    def conv_four(st):
        @pl.when(st.pos1 == 0)
        def _():
            for e in range(events):
                @pl.when(st.pos2 != e)
                def _(e=e):
                    conv3_copy(st, 1, e).wait_recv()
            for d in range(1, n):
                conv4_copy(st, d).start()

    def conv_five(st):
        @pl.when(st.pos1 != 0)
        def _():
            copy_to(st.conv, st.conv, sc4.at[st.index, 0], rc4.at[st.index], st.peer1(0)).wait_recv()

    def rs2_copy(st, d):
        k = lax.rem(st.pos2 + d, n)
        return copy_to(
            st.red.at[k], st.cand2.at[st.pos2], s2.at[st.index, d - 1], r2.at[st.index, d - 1], st.peer2(k)
        )

    def rs_two(st):
        for d in range(1, n):
            rs1_wait(st, d)
        loads[1 + st.index].wait()
        for e in range(events):
            p, _, row = owner(st, e)
            for u in range(per_event):
                st.red[e * per_event + u] = st.cand[p, row, u * piece : (u + 1) * piece, :]
        for d in range(1, n):
            rs2_copy(st, d).start()
        st.cand2[st.pos2] = st.red[st.pos2]

    def place(head, k):
        return pool.at[base + k // per_event, head, pl.ds(pl.multiple_of(lax.rem(k, per_event) * piece, piece), piece)]

    def ag1_copy(st, d):
        k = lax.rem(st.pos2 + d, n)
        spot = place(st.index * n + st.pos1, st.pos2)
        return copy_to(spot, spot, s3.at[st.index, d - 1], r3.at[st.index, d - 1], st.peer2(k))

    def ag1_wait(st, d):
        k = lax.rem(st.pos2 + n - d, n)
        spot = place(st.index * n + st.pos1, k)
        copy_to(spot, spot, s3.at[st.index, d - 1], r3.at[st.index, d - 1], st.peer2(k)).wait_recv()

    def ag_one(st):
        for d in range(1, n):
            k = lax.rem(st.pos2 + n - d, n)
            copy_to(
                st.cand2.at[k], st.cand2.at[k], s2.at[st.index, d - 1], r2.at[st.index, d - 1], st.peer2(k)
            ).wait_recv()
        _, q, _ = owner(st, st.pos2 // per_event)
        place(st.index * n + st.pos1, st.pos2)[...] = st.cand2[q]
        for d in range(1, n):
            ag1_copy(st, d).start()

    def ring_copy(st, s, way):
        first, last = base, base + events
        if s == n // 2 - 1:
            middle = base + events // 2
            first, last = (first, middle) if way == 0 else (middle, last)
        if way == 0:
            chunk, target = lax.rem(st.pos1 + n - s, n), lax.rem(st.pos1 + 1, n)
        else:
            chunk, target = lax.rem(st.pos1 + s, n), lax.rem(st.pos1 + n - 1, n)
        spot = pool.at[first:last, st.index * n + chunk]
        return copy_to(spot, spot, s4.at[st.index, way, s], r4.at[st.index, way, s], st.peer1(target))

    def ring_wait(st, s, way):
        first, last = base, base + events
        if s == n // 2 - 1:
            middle = base + events // 2
            first, last = (first, middle) if way == 0 else (middle, last)
        chunk = lax.rem(st.pos1 + (n - 1 - s if way == 0 else s + 1), n)
        spot = pool.at[first:last, st.index * n + chunk]
        copy_to(spot, spot, s4.at[st.index, way, s], r4.at[st.index, way, s], st.peer1(chunk)).wait_recv()

    for st in streams:
        conv_two(st)
    for st in streams:
        rs_two(st)
    for st in streams:
        conv_three(st)
    for st in streams:
        ag_one(st)
    for st in streams:
        conv_four(st)
    for st in streams:
        for d in range(1, n):
            ag1_wait(st, d)
        for way in range(2):
            ring_copy(st, 0, way).start()

    for st in streams:
        conv_five(st)
    move_copies[0].wait_recv()
    sources = [(base + e, e) for e in range(events)]

    def unpack(row, top, bottom):
        both = (top.astype(F32), bottom.astype(F32))
        for tap in range(tail):
            for j in range(wrows):
                r = tap * wrows + j
                ucf[row, tap : tap + 1, j * 128 : (j + 1) * 128] = both[r // 16][r % 16 : r % 16 + 1]
            for j in range(grows):
                r = tail * wrows + tap * grows + j
                ucf[row, tap : tap + 1, width + j * 128 : width + (j + 1) * 128] = both[r // 16][r % 16 : r % 16 + 1]

    for row, e in sources:
        unpack(row, conv_a[e], conv_b[e])
    unpack(slots, camec[0:16], camec[16:32])

    index = []
    for s in range(slots):
        e = se_ref[s]
        at = jnp.where(e >= 0, base + e, jnp.where(moved == s, slots, s))
        index.append(at)
        rows = ucf[at]
        for tap in range(tail):
            join[tap, s : s + 1, :] = rows[tap : tap + 1, 0:width]
            joing[tap, s : s + 1, :] = rows[tap : tap + 1, width : width + gw]

    for st in streams:
        for way in range(2):
            ring_wait(st, 0, way)
            ring_copy(st, 1, way).start()

    for t in range(steps):
        v = ibias_ref[...].astype(F32)
        g = gbias_ref[...].astype(F32)
        for k in range(taps):
            v = v + ikern_ref[k : k + 1, :].astype(F32) * join[t + k]
            g = g + gkern_ref[k : k + 1, :].astype(F32) * joing[t + k]
        xs[t] = silu(v)
        gs[t] = silu(g)

    which = lax.broadcasted_iota(jnp.int32, (heads, width), 1) // hsize
    expand = (which == lax.broadcasted_iota(jnp.int32, (heads, width), 0)).astype(BF16)

    def widen(v):
        high, low = split2(v)
        return jnp.dot(high, expand, preferred_element_type=F32) + jnp.dot(low, expand, preferred_element_type=F32)

    for t in range(steps):
        c = gs[t, :, state:gw]
        for s in range(t + 1):
            dot = jnp.sum(c * gs[s, :, 0:state], axis=-1, keepdims=True)
            m = (step[s] if s == t else jnp.exp(decay[t] - decay[s]) * step[s]) * dot
            ms[s] = m + skip_ref[...] if s == t else m
        ms[t + 1] = jnp.exp(decay[t])
        ms[t + 2] = jnp.exp(decay[steps - 1] - decay[t]) * step[t]
        rows = ms[0 : t + 3].reshape(((t + 3) * 8, heads))
        wide = widen(rows).reshape((t + 3, 8, width))
        y = wide[0] * xs[0]
        for s in range(1, t + 1):
            y = y + wide[s] * xs[s]
        ys[t] = y
        es[t] = wide[t + 1]
        us[t] = wide[t + 2] * xs[t]

    for s in range(1, n // 2 - 1):
        for st in streams:
            for way in range(2):
                ring_wait(st, s, way)
                ring_copy(st, s + 1, way).start()

    eye = lax.broadcasted_iota(jnp.int32, (heads, heads), 0) == lax.broadcasted_iota(jnp.int32, (heads, heads), 1)
    last = jnp.exp(decay[steps - 1])
    diag = jnp.concatenate([jnp.where(eye, last[s : s + 1], 0.0) for s in range(slots)], axis=0)
    kept = jnp.dot(diag, jnp.ones((heads, state), F32), precision=lax.Precision.HIGHEST, preferred_element_type=F32)

    for st in streams:
        for way in range(2):
            ring_wait(st, n // 2 - 1, way)
    move_copies[1].wait_recv()

    pad = jnp.zeros((16 - steps, state), F32)
    padw = jnp.zeros((16 - steps, width), F32)
    for s in range(slots):
        start = pool[index[s]].reshape((width, state))
        c_high, c_low = split2(jnp.concatenate([gs[:, s, state:gw], pad], axis=0))
        read = lax.dot_general(
            jnp.concatenate([c_high, c_low], axis=0), start, (((1,), (1,)), ((), ())), preferred_element_type=F32
        )
        read = read[0:steps] + read[16 : 16 + steps]
        ys[:, s, :] = ys[:, s, :] + es[:, s, :] * read
        b_high, b_low = split2(jnp.concatenate([gs[:, s, 0:state], pad], axis=0))
        u_high, u_low = split2(jnp.concatenate([us[:, s, :], padw], axis=0))
        added = lax.dot_general(
            jnp.concatenate([u_high, u_low, u_high], axis=0),
            jnp.concatenate([b_high, b_high, b_low], axis=0),
            (((0,), (0,)), ((), ())), preferred_element_type=F32,
        )
        for h in range(heads):
            rows = slice(h * hsize, (h + 1) * hsize)
            k = s * heads + h
            fin_ref[s, h] = (kept[k : k + 1] * start[rows].astype(F32) + added[rows]).astype(BF16)

    for t in range(steps):
        y = ys[t, 0:slots, :] * silu(gate_ref[t].astype(F32))
        mean = jnp.sum(y * y, axis=-1, keepdims=True) / width
        out_ref[t] = (y * lax.rsqrt(mean + EPSILON) * gain_ref[...]).astype(BF16)

    for st in streams:
        @pl.when(st.pos1 != 0)
        def _(st=st):
            conv1_copy(st, 1).wait_send()

        @pl.when(st.pos1 == 0)
        def _(st=st):
            for k in range(events):
                @pl.when(st.pos2 != k)
                def _(k=k):
                    conv2_copy(st, k).wait_send()

                @pl.when(st.pos2 == k)
                def _(k=k):
                    for d in range(1, n):
                        conv3_copy(st, d, k).wait_send()
            for d in range(1, n):
                conv4_copy(st, d).wait_send()

        for d in range(1, n):
            rs1_copy(st, d).wait_send()
            rs2_copy(st, d).wait_send()
            ag1_copy(st, d).wait_send()
        for s in range(n // 2):
            for way in range(2):
                ring_copy(st, s, way).wait_send()
    for copy in move_copies:
        copy.wait_send()


def on_device(
    n,
    inner_input, group_input, gate_input, step_size, scan_state, conv_inner, conv_group,
    prefix_scan, prefix_inner, prefix_group, inner_kernel, inner_bias, group_kernel, group_bias,
    decay_rate, step_bias, skip_gain, norm_gain, event_prefix, slot_event, moved_slot,
):
    slots, steps, width = inner_input.shape
    pref, heads, hsize, state = prefix_scan.shape
    events = event_prefix.shape[0]
    taps = inner_kernel.shape[0]
    tail = taps - 1
    gw = group_input.shape[-1]
    piece = events * hsize // n
    final_inner = inner_input[:, steps - tail :]
    final_group = group_input[:, steps - tail :]

    args = (
        inner_input.transpose(1, 0, 2),
        group_input.reshape(slots, steps, gw).transpose(1, 0, 2),
        gate_input.transpose(1, 0, 2),
        step_size.transpose(1, 0, 2),
        scan_state,
        conv_inner,
        conv_group.reshape(slots, tail, gw),
        prefix_scan,
        prefix_inner.transpose(1, 0, 2),
        prefix_group.reshape(pref, tail, gw).transpose(1, 0, 2),
        inner_kernel,
        inner_bias.reshape(1, width),
        group_kernel.reshape(taps, gw),
        group_bias.reshape(1, gw),
        decay_rate.reshape(1, heads),
        step_bias.reshape(1, heads),
        skip_gain.reshape(1, heads),
        norm_gain.reshape(1, width),
        event_prefix,
        slot_event,
        moved_slot,
    )
    vmem = pl.BlockSpec(memory_space=pltpu.VMEM)
    smem = pl.BlockSpec(memory_space=pltpu.SMEM)
    hbm = pl.BlockSpec(memory_space=pl.ANY)
    specs = [vmem] * len(args)
    specs[4] = specs[7] = hbm
    specs[-3:] = [smem] * 3
    dma = pltpu.SemaphoreType.DMA
    block = (hsize, state)
    scratch = [
        pltpu.VMEM((slots + 1 + events, heads) + block, BF16),
        pltpu.VMEM((heads,) + block, BF16),
        pltpu.VMEM((n, pref) + block, BF16),
        pltpu.VMEM((n, pref) + block, BF16),
        pltpu.VMEM((n, piece, state), BF16),
        pltpu.VMEM((n, piece, state), BF16),
        pltpu.VMEM((n, piece, state), BF16),
        pltpu.VMEM((n, piece, state), BF16),
        pltpu.VMEM((pref + 1, 32, 128), F32),
        pltpu.VMEM((pref + 1, 32, 128), BF16),
        pltpu.VMEM((n, pref, 16, 128), BF16),
        pltpu.VMEM((n, pref, 16, 128), BF16),
        pltpu.VMEM((events, 16, 128), BF16),
        pltpu.VMEM((events, 16, 128), BF16),
        pltpu.VMEM((n, 16, 128), BF16),
        pltpu.VMEM((n, 16, 128), BF16),
        pltpu.VMEM((events, 16, 128), BF16),
        pltpu.VMEM((events, 16, 128), BF16),
        pltpu.VMEM((32, 128), BF16),
        pltpu.VMEM((slots + 1 + events, tail, width + gw), F32),
        pltpu.VMEM((steps + tail, 8, width), F32),
        pltpu.VMEM((steps + tail, 8, gw), F32),
        pltpu.VMEM((steps, 8, width), F32),
        pltpu.VMEM((steps, 8, gw), F32),
        pltpu.VMEM((steps, 8, heads), F32),
        pltpu.VMEM((steps + 2, 8, heads), F32),
        pltpu.VMEM((steps, 8, width), F32),
        pltpu.VMEM((steps, 8, width), F32),
        pltpu.VMEM((steps, 8, width), F32),
        dma((3,)),
        dma((2, n - 1)), dma((2, n - 1)),
        dma((2, n - 1)), dma((2, n - 1)),
        dma((2, n - 1)), dma((2, n - 1)),
        dma((2, 2, n // 2)), dma((2, 2, n // 2)),
        dma((2,)), dma((2, n - 1)),
        dma((2, events)), dma((2, n)),
        dma((2, n - 1)), dma((2, events)),
        dma((2, n - 1)), dma((2,)),
        dma((2,)), dma((2,)),
    ]
    layer, final_scan = pl.pallas_call(
        functools.partial(kernel, n, slots, pref, events, steps, heads, hsize, state),
        out_shape=(
            jax.ShapeDtypeStruct((steps, slots, width), BF16),
            jax.ShapeDtypeStruct(scan_state.shape, BF16),
        ),
        in_specs=specs,
        out_specs=(vmem, vmem),
        scratch_shapes=scratch,
        compiler_params=pltpu.CompilerParams(
            collective_id=0, has_side_effects=True, vmem_limit_bytes=40 * 1024 * 1024
        ),
    )(*args)
    return layer.transpose(1, 0, 2), final_scan, final_inner, final_group


def solution(mesh):
    count = mesh.shape["rep"]
    n = 1
    while n * n < count:
        n += 1
    placed = (
        P("rep", None, "ch"),
        P("rep", None, "ch", None),
        P("rep", None, "ch"),
        P("rep", None, "ch"),
        P("rep", "ch", None, None),
        P("rep", None, "ch"),
        P("rep", None, "ch", None),
        P("rep", "ch", None, None),
        P("rep", None, "ch"),
        P("rep", None, "ch", None),
        P(None, "ch"),
        P("ch"),
        P(None, "ch", None),
        P("ch", None),
        P("ch"),
        P("ch"),
        P("ch"),
        P("ch"),
        P(),
        P("rep"),
        P("rep"),
    )
    return jax.shard_map(
        functools.partial(on_device, n),
        mesh=mesh,
        in_specs=placed,
        out_specs=(
            P("rep", None, "ch"),
            P("rep", "ch", None, None),
            P("rep", None, "ch"),
            P("rep", None, "ch", None),
        ),
        check_vma=False,
    )
```

```python
import functools

import jax
import jax.numpy as jnp
from jax import lax
from jax.experimental import pallas as pl
from jax.experimental.pallas import tpu as pltpu
from jax.sharding import PartitionSpec as P

MESH = pl.DeviceIdType.MESH
BF16 = jnp.bfloat16
F32 = jnp.float32
EPSILON = 1e-05
PARTS = 1
MOVES = (((0, 0), (0, 1)), ((0, 2), (0, 3)), (), ())


def silu(v):
    return v / (1.0 + jnp.exp(-v))


def split2(v):
    high = v.astype(BF16)
    low = (v - high.astype(F32)).astype(BF16)
    return high, low


class Stream:
    def __init__(self, index, pos1, pos2, peer1, peer2, cand, red, cand2, candc, redc, candc2, conv):
        self.index = index
        self.pos1, self.pos2 = pos1, pos2
        self.peer1, self.peer2 = peer1, peer2
        self.cand, self.red, self.cand2 = cand, red, cand2
        self.candc, self.redc, self.candc2 = candc, redc, candc2
        self.conv = conv


def kernel(
    n, parts, slots, pref, events, steps, heads, hsize, state,
    *refs,
):
    inputs, refs = refs[:21], refs[21:]
    (out_ref, fin_ref, finner_ref, fgroup_ref), refs = refs[:4], refs[4:]
    held, refs = refs[:19], refs[19:]
    scan_hbm, pscan_hbm = inputs[4], inputs[7]
    (
        inner_ref, group_ref, gate_ref, dt_ref, cinner_ref, cgroup_ref, pinner_ref, pgroup_ref,
        ikern_ref, ibias_ref, gkern_ref, gbias_ref, decay_ref, dbias_ref, skip_ref, gain_ref, ep_ref, se_ref, mv_ref,
    ) = held
    blocks, refs = refs[: 8 * parts], refs[8 * parts :]
    cands, reds, cand2s = (blocks[2 * parts * i : 2 * parts * (i + 1)] for i in range(3))
    pools, stages = blocks[6 * parts : 7 * parts], blocks[7 * parts :]
    (
        pkf, pkb, candc_a, candc_b, redc_a, redc_b, candc2_a, candc2_b, conv_a, conv_b, camec, ucf,
        join, joing, xs, gs, dts, ms, us, ys, es,
        load_sem, small_sem, s1, r1, s2, r2, s3, r3, s4, r4, sc1, rc1, sc2, rc2, sc3, rc3, sc4, rc4, sm, rm,
    ) = refs
    rep = lax.axis_index("rep")
    total = n * n
    py = lax.rem(rep, n)
    pz = rep // n
    width = heads * hsize
    wrows = width // 128
    gw = 2 * state
    grows = gw // 128
    part = heads * hsize // parts
    share = part // 2
    chunk = share // n
    piece = events * chunk // n
    per_event = n // events
    base = slots + 1
    taps = ikern_ref.shape[0]
    tail = taps - 1

    def to(r):
        return {"rep": r}

    right = lax.rem(rep + 1, total)
    left = lax.rem(rep + total - 1, total)

    barrier = pltpu.get_barrier_semaphore()
    for d in range(1, n):
        pl.semaphore_signal(barrier, inc=1, device_id=to(pz * n + lax.rem(py + d, n)), device_id_type=MESH)
        pl.semaphore_signal(barrier, inc=1, device_id=to(lax.rem(pz + d, n) * n + py), device_id_type=MESH)
    pl.semaphore_signal(barrier, inc=1, device_id=to(right), device_id_type=MESH)
    pl.semaphore_signal(barrier, inc=1, device_id=to(left), device_id_type=MESH)

    def chunk_rows(st, j):
        return pl.ds(pl.multiple_of(st * share + j * chunk, chunk), chunk)

    def all_rows(b, st, j):
        return pl.ds(pl.multiple_of(b * part + st * share + j * chunk, chunk), chunk)

    first = (6, 7, 4, 5, 18)
    rest = [v for i, v in enumerate(inputs) if i not in (4, 7)]
    small = [pltpu.make_async_copy(src, dst, small_sem.at[i]) for i, (src, dst) in enumerate(zip(rest, held))]
    for i in first:
        small[i].start()
    scan_loads = [
        pltpu.make_async_copy(
            scan_hbm.at[:, b * part : (b + 1) * part], pools[b].at[0:slots], load_sem.at[2 * parts + b]
        )
        for b in range(parts)
    ]
    for copy in scan_loads:
        copy.start()
    own_loads = {}
    for b in range(parts):
        for i, pos in enumerate((py, pz)):
            at = i * parts + b
            own_loads[i, b] = pltpu.make_async_copy(
                pscan_hbm.at[:, all_rows(b, i, pos)], cands[at].at[pos], load_sem.at[at]
            )
            own_loads[i, b].start()
    for i, copy in enumerate(small):
        if i not in first:
            copy.start()

    def copy_to(src, dst, send, recv, device):
        return pltpu.make_async_remote_copy(
            src_ref=src, dst_ref=dst, send_sem=send, recv_sem=recv, device_id=to(device), device_id_type=MESH
        )

    streams = (
        Stream(0, py, pz, lambda j: pz * n + j, lambda k: k * n + py,
               cands[:parts], reds[:parts], cand2s[:parts], candc_a, redc_a, candc2_a, conv_a),
        Stream(1, pz, py, lambda j: j * n + py, lambda k: pz * n + k,
               cands[parts:], reds[parts:], cand2s[parts:], candc_b, redc_b, candc2_b, conv_b),
    )

    def owner(st, e):
        rid = ep_ref[e]
        r = rid // pref
        y, z = lax.rem(r, n), r // n
        return (y, z, lax.rem(rid, pref)) if st.index == 0 else (z, y, lax.rem(rid, pref))

    def half(i):
        return slice(i * 16, (i + 1) * 16)

    def conv1_copy(st):
        return copy_to(
            pkb.at[0:pref, half(st.index)], st.candc.at[st.pos1], sc1.at[st.index], rc1.at[st.index], st.peer1(0)
        )

    def taken(ref, sem, way):
        copy = copy_to(ref, ref, sem, sem, right)
        copy.wait_send() if way == 0 else copy.wait_recv()

    def rs1_copy(st, b, d):
        j = lax.rem(st.pos1 + d, n)
        return copy_to(
            pscan_hbm.at[:, all_rows(b, st.index, j)], st.cand[b].at[st.pos1],
            s1.at[st.index, b], r1.at[st.index, b], st.peer1(j),
        )

    far_first = (n // 2, *[x for k in range(n // 2 - 1, 0, -1) for x in (k, n - k)])
    pl.semaphore_wait(barrier, 2 * (n - 1) + 2)

    def rs1_send(b):
        for d in far_first:
            for st in streams:
                rs1_copy(st, b, d).start()

    for b in range(parts):
        rs1_send(b)

    pkf[...] = jnp.zeros_like(pkf)
    for i in first:
        small[i].wait()
    moved = mv_ref[0]

    def pack(slot, inner_rows, group_rows):
        for tap in range(tail):
            for j in range(wrows):
                pkf[slot, tap * wrows + j : tap * wrows + j + 1, :] = inner_rows[tap][:, j * 128 : (j + 1) * 128]
            for j in range(grows):
                r = tail * wrows + tap * grows + j
                pkf[slot, r : r + 1, :] = group_rows[tap][:, j * 128 : (j + 1) * 128]

    p_inner = [pinner_ref[tap].astype(F32) for tap in range(tail)]
    p_group = [pgroup_ref[tap].astype(F32) for tap in range(tail)]
    for q in range(pref):
        pack(q, [v[q : q + 1] for v in p_inner], [v[q : q + 1] for v in p_group])
    m_inner = cinner_ref[moved].astype(F32)
    m_group = cgroup_ref[moved].astype(F32)
    pack(pref, [m_inner[t : t + 1] for t in range(tail)], [m_group[t : t + 1] for t in range(tail)])
    pkb[...] = pkf[...].astype(BF16)

    for st in streams:
        @pl.when(st.pos1 != 0)
        def _(st=st):
            conv1_copy(st).start()

    for b in range(parts):
        scan_loads[b].wait()
        for q in range(0, part, hsize):
            rows = slice(q, q + hsize)
            got = pools[b][0, rows]
            for s in range(1, slots):
                got = jnp.where(moved == s, pools[b][s, rows], got)
            stages[b][rows] = got
    conv_move = copy_to(pkb.at[pref], camec, sm.at[parts], rm.at[parts], right)
    conv_move.start()

    def move(b, i, count):
        rows = pl.ds(i * part // count, part // count)
        return copy_to(stages[b].at[rows], pools[b].at[slots, rows], sm.at[b], rm.at[b], right)

    for i, copy in enumerate(small):
        if i not in first:
            copy.wait()
    join[...] = jnp.zeros_like(join)
    joing[...] = jnp.zeros_like(joing)
    dts[...] = jnp.zeros_like(dts)
    for t in range(steps):
        join[tail + t, 0:slots, :] = inner_ref[t].astype(F32)
        joing[tail + t, 0:slots, :] = group_ref[t].astype(F32)
        if t >= steps - tail:
            for s in range(slots):
                k = t - (steps - tail)
                finner_ref[s, k : k + 1, :] = inner_ref[t, s : s + 1, :]
                fgroup_ref[s, k : k + 1, :] = group_ref[t, s : s + 1, :]
        dts[t, 0:slots, :] = dt_ref[t]
    for s in range(slots):
        ucf[s, :, 0:width] = cinner_ref[s].astype(F32)
        ucf[s, :, width : width + gw] = cgroup_ref[s].astype(F32)
    step = []
    decay = []
    for t in range(steps):
        v = dts[t] + dbias_ref[...]
        v = jnp.maximum(v, 0.0) + jnp.log1p(jnp.exp(-jnp.abs(v)))
        step.append(v)
        fall = -v * decay_ref[...]
        decay.append(fall if t == 0 else decay[-1] + fall)

    def conv2_copy(st, k):
        return copy_to(
            st.redc.at[k], st.candc2.at[st.pos2], sc2.at[st.index], rc2.at[st.index], st.peer2(k)
        )

    def conv_two(st):
        @pl.when(st.pos1 == 0)
        def _():
            taken(st.candc.at[1:n], rc1.at[st.index], 1)
            st.candc[0] = pkb[0:pref, half(st.index)]
            for e in range(events):
                p, _, row = owner(st, e)
                st.redc[e] = st.candc[p, row]
            for k in range(events):
                @pl.when(st.pos2 != k)
                def _(k=k):
                    conv2_copy(st, k).start()

                @pl.when(st.pos2 == k)
                def _(k=k):
                    st.candc2[k] = st.redc[k]

    def conv3_copy(st, d, e):
        k = lax.rem(st.pos2 + d, n)
        return copy_to(st.conv.at[e], st.conv.at[e], sc3.at[st.index], rc3.at[st.index], st.peer2(k))

    def conv_three(st):
        @pl.when(st.pos1 == 0)
        def _():
            for e in range(events):
                @pl.when(st.pos2 == e)
                def _(e=e):
                    taken(st.candc2.at[0 : n - 1], rc2.at[st.index], 1)
                    _, q, _ = owner(st, e)
                    st.conv[e] = st.candc2[q]
                    for d in range(1, n):
                        conv3_copy(st, d, e).start()

    def conv4_copy(st, d):
        j = lax.rem(st.pos1 + d, n)
        return copy_to(st.conv, st.conv, sc4.at[st.index], rc4.at[st.index], st.peer1(j))

    def conv_four(st):
        @pl.when(st.pos1 == 0)
        def _():
            @pl.when(st.pos2 < events)
            def _():
                taken(st.conv.at[0 : events - 1], rc3.at[st.index], 1)

            @pl.when(st.pos2 >= events)
            def _():
                taken(st.conv, rc3.at[st.index], 1)

            for d in range(1, n):
                conv4_copy(st, d).start()

    def conv_five(st):
        @pl.when(st.pos1 != 0)
        def _():
            taken(st.conv, rc4.at[st.index], 1)

    def rs2_copy(st, b, d):
        k = lax.rem(st.pos2 + d, n)
        return copy_to(
            st.red[b].at[k], st.cand2[b].at[st.pos2], s2.at[st.index, b], r2.at[st.index, b], st.peer2(k)
        )

    def rs_two(st, b):
        taken(st.cand[b].at[0 : n - 1], r1.at[st.index, b], 1)
        own_loads[st.index, b].wait()
        for e in range(events):
            p, _, row = owner(st, e)
            for u in range(per_event):
                st.red[b][e * per_event + u] = st.cand[b][p, row, u * piece : (u + 1) * piece, :]
        for d in far_first:
            rs2_copy(st, b, d).start()
        st.cand2[b][st.pos2] = st.red[b][st.pos2]

    def place(b, st, j, k):
        offset = pl.multiple_of(st.index * share + j * chunk + lax.rem(k, per_event) * piece, piece)
        return pools[b].at[base + k // per_event, pl.ds(offset, piece)]

    def ag1_copy(st, b, d):
        spot = place(b, st, st.pos1, st.pos2)
        return copy_to(spot, spot, s3.at[st.index, b], r3.at[st.index, b], st.peer2(lax.rem(st.pos2 + d, n)))

    def ag_one(st, b):
        taken(st.cand2[b].at[0 : n - 1], r2.at[st.index, b], 1)
        _, q, _ = owner(st, st.pos2 // per_event)
        place(b, st, st.pos1, st.pos2)[...] = st.cand2[b][q]
        for d in far_first:
            ag1_copy(st, b, d).start()

    pair = events // 2
    whole = (0, events)
    first_leg = [(0, 2) + whole, (0, -2) + whole, (0, 1) + whole, (0, -1) + whole]
    second_leg = [(-2, 2, 0, pair), (-2, 1) + whole, (2, -2, pair, events), (2, -1) + whole]
    if n == 4:
        first_leg = [(0, 2, 0, pair), (0, -2, pair, events), (0, 1) + whole, (0, -1) + whole]
        second_leg = []
    legs = first_leg + second_leg

    def leg_spot(st, b, distance, first, last):
        j = lax.rem(st.pos1 + n + distance, n)
        return pools[b].at[base + first : base + last, chunk_rows(st.index, j)]

    def leg_send(st, b, some):
        for i in some:
            c, t, a, z = legs[i]
            spot = leg_spot(st, b, c, a, z)
            target = st.peer1(lax.rem(st.pos1 + n + t, n))
            copy_to(spot, spot, s4.at[st.index, b], r4.at[st.index, b, i], target).start()

    def leg_wait(st, b, some):
        for i in some:
            c, t, a, z = legs[i]
            taken(leg_spot(st, b, c - t, a, z), r4.at[st.index, b, i], 1)

    def spread(st, b):
        taken(st.cand2[b].at[0 : n - 1], r3.at[st.index, b], 1)
        leg_send(st, b, range(4))

    def hand_on(b):
        if second_leg:
            for way in range(2):
                for st in streams:
                    leg_wait(st, b, [way])
                    leg_send(st, b, [4 + 2 * way, 5 + 2 * way])

    def arrive(b):
        for st in streams:
            leg_wait(st, b, range(2 if second_leg else 0, len(legs)))

    def each(phase, b):
        for st in streams:
            phase(st, b)

    def conv(phase):
        for st in streams:
            phase(st)

    def moves(when):
        for b, i in MOVES[when]:
            move(b, i, 4 // parts).start()

    for when, (phase, conv_phase) in enumerate(((rs_two, conv_two), (ag_one, conv_three), (spread, conv_four))):
        for b in range(parts):
            each(phase, b)
            if b == 0:
                conv(conv_phase)
        moves(when)
    for b in range(parts):
        hand_on(b)
    moves(3)
    conv(conv_five)
    conv_move.wait_recv()
    sources = [(base + e, e) for e in range(events)]

    def unpack(row, top, bottom):
        both = (top.astype(F32), bottom.astype(F32))
        for tap in range(tail):
            for j in range(wrows):
                r = tap * wrows + j
                ucf[row, tap : tap + 1, j * 128 : (j + 1) * 128] = both[r // 16][r % 16 : r % 16 + 1]
            for j in range(grows):
                r = tail * wrows + tap * grows + j
                ucf[row, tap : tap + 1, width + j * 128 : width + (j + 1) * 128] = both[r // 16][r % 16 : r % 16 + 1]

    for row, e in sources:
        unpack(row, conv_a[e], conv_b[e])
    unpack(slots, camec[0:16], camec[16:32])

    index = []
    for s in range(slots):
        e = se_ref[s]
        at = jnp.where(e >= 0, base + e, jnp.where(moved == s, slots, s))
        index.append(at)
        rows = ucf[at]
        for tap in range(tail):
            join[tap, s : s + 1, :] = rows[tap : tap + 1, 0:width]
            joing[tap, s : s + 1, :] = rows[tap : tap + 1, width : width + gw]


    for t in range(steps):
        v = ibias_ref[...].astype(F32).reshape(1, width)
        g = gbias_ref[...].astype(F32)
        for k in range(taps):
            v = v + ikern_ref[k : k + 1, :].astype(F32) * join[t + k]
            g = g + gkern_ref[k : k + 1, :].astype(F32) * joing[t + k]
        xs[t] = silu(v)
        gs[t] = silu(g)

    which = lax.broadcasted_iota(jnp.int32, (heads, width), 1) // hsize
    expand = (which == lax.broadcasted_iota(jnp.int32, (heads, width), 0)).astype(BF16)

    def widen(v):
        high, low = split2(v)
        return jnp.dot(high, expand, preferred_element_type=F32) + jnp.dot(low, expand, preferred_element_type=F32)

    for t in range(steps):
        c = gs[t, :, state:gw]
        for s in range(t + 1):
            dot = jnp.sum(c * gs[s, :, 0:state], axis=-1, keepdims=True)
            m = (step[s] if s == t else jnp.exp(decay[t] - decay[s]) * step[s]) * dot
            ms[s] = m + skip_ref[...] if s == t else m
        ms[t + 1] = jnp.exp(decay[t])
        ms[t + 2] = jnp.exp(decay[steps - 1] - decay[t]) * step[t]
        rows = ms[0 : t + 3].reshape(((t + 3) * 8, heads))
        wide = widen(rows).reshape((t + 3, 8, width))
        y = wide[0] * xs[0]
        for s in range(1, t + 1):
            y = y + wide[s] * xs[s]
        ys[t] = y
        es[t] = wide[t + 1]
        us[t] = wide[t + 2] * xs[t]

    eye = lax.broadcasted_iota(jnp.int32, (heads, heads), 0) == lax.broadcasted_iota(jnp.int32, (heads, heads), 1)
    last = jnp.exp(decay[steps - 1])
    diag = jnp.concatenate([jnp.where(eye, last[s : s + 1], 0.0) for s in range(slots)], axis=0)
    kept = jnp.dot(diag, jnp.ones((heads, state), F32), precision=lax.Precision.HIGHEST, preferred_element_type=F32)

    pad = jnp.zeros((16 - steps, state), F32)
    padw = jnp.zeros((16 - steps, part), F32)
    for b in range(parts):
        arrive(b)
        taken(stages[b], rm.at[b], 1)
        lanes = slice(b * part, (b + 1) * part)
        for s in range(slots):
            start = pools[b][index[s]]
            c_high, c_low = split2(jnp.concatenate([gs[:, s, state:gw], pad], axis=0))
            read = lax.dot_general(
                jnp.concatenate([c_high, c_low], axis=0), start, (((1,), (1,)), ((), ())), preferred_element_type=F32
            )
            read = read[0:steps] + read[16 : 16 + steps]
            ys[:, s, lanes] = ys[:, s, lanes] + es[:, s, lanes] * read
            b_high, b_low = split2(jnp.concatenate([gs[:, s, 0:state], pad], axis=0))
            u_high, u_low = split2(jnp.concatenate([us[:, s, lanes], padw], axis=0))
            added = lax.dot_general(
                jnp.concatenate([u_high, u_low, u_high], axis=0),
                jnp.concatenate([b_high, b_high, b_low], axis=0),
                (((0,), (0,)), ((), ())), preferred_element_type=F32,
            )
            for q in range(part // hsize):
                rows = slice(q * hsize, (q + 1) * hsize)
                h = b * (part // hsize) + q
                k = s * heads + h
                fin_ref[s, h] = (kept[k : k + 1] * start[rows].astype(F32) + added[rows]).astype(BF16)

    for t in range(steps):
        y = ys[t, 0:slots, :] * silu(gate_ref[t].astype(F32))
        mean = jnp.sum(y * y, axis=-1, keepdims=True) / width
        out_ref[t] = (y * lax.rsqrt(mean + EPSILON) * gain_ref[...]).astype(BF16)

    for st in streams:
        @pl.when(st.pos1 != 0)
        def _(st=st):
            conv1_copy(st).wait_send()

        @pl.when(st.pos1 == 0)
        def _(st=st):
            @pl.when(st.pos2 < events)
            def _():
                taken(st.conv.at[0 : events - 1], sc2.at[st.index], 0)
                taken(st.candc2.at[0 : n - 1], sc3.at[st.index], 0)

            @pl.when(st.pos2 >= events)
            def _():
                taken(st.conv, sc2.at[st.index], 0)

            taken(pools[0].at[base, 0 : (n - 1) * events * 16], sc4.at[st.index], 0)

        for b in range(parts):
            taken(st.cand[b].at[0 : n - 1], s1.at[st.index, b], 0)
            taken(st.red[b].at[0 : n - 1], s2.at[st.index, b], 0)
            taken(st.red[b].at[0 : n - 1], s3.at[st.index, b], 0)
            taken(pools[b].at[base : base + events, 0 : (n - 1) * chunk], s4.at[st.index, b], 0)
    conv_move.wait_send()
    for b in range(parts):
        taken(stages[b], sm.at[b], 0)


def finish(*refs):
    half = len(refs) // 2
    copies = [pltpu.make_async_copy(a, b, refs[-1].at[i]) for i, (a, b) in enumerate(zip(refs[:half], refs[half:-1]))]
    for copy in copies:
        copy.start()
    for copy in copies:
        copy.wait()


def on_device(
    n,
    inner_input, group_input, gate_input, step_size, scan_state, conv_inner, conv_group,
    prefix_scan, prefix_inner, prefix_group, inner_kernel, inner_bias, group_kernel, group_bias,
    decay_rate, step_bias, skip_gain, norm_gain, event_prefix, slot_event, moved_slot,
):
    slots, steps, width = inner_input.shape
    pref, heads, hsize, state = prefix_scan.shape
    events = event_prefix.shape[0]
    taps = inner_kernel.shape[0]
    tail = taps - 1
    gw = group_input.shape[-1]
    part = heads * hsize // PARTS
    chunk = part // (2 * n)
    piece = events * chunk // n

    args = (
        inner_input.transpose(1, 0, 2),
        group_input.reshape(slots, steps, gw).transpose(1, 0, 2),
        gate_input.transpose(1, 0, 2),
        step_size.transpose(1, 0, 2),
        scan_state.reshape(slots, width, state),
        conv_inner,
        conv_group.reshape(slots, tail, gw),
        prefix_scan.reshape(pref, width, state),
        prefix_inner.transpose(1, 0, 2),
        prefix_group.reshape(pref, tail, gw).transpose(1, 0, 2),
        inner_kernel,
        inner_bias,
        group_kernel.reshape(taps, gw),
        group_bias.reshape(1, gw),
        decay_rate.reshape(1, heads),
        step_bias.reshape(1, heads),
        skip_gain.reshape(1, heads),
        norm_gain.reshape(1, width),
        event_prefix,
        slot_event,
        moved_slot,
    )
    vmem = pl.BlockSpec(memory_space=pltpu.VMEM)
    hbm = pl.BlockSpec(memory_space=pl.ANY)
    specs = [hbm] * len(args)
    small = [v for i, v in enumerate(args) if i not in (4, 7)]
    args = tuple(v if v.size == 1 else pltpu.with_memory_space_constraint(v, pltpu.HBM) for v in args)
    dma = pltpu.SemaphoreType.DMA
    scratch = [(pltpu.VMEM if i < len(small) - 3 else pltpu.SMEM)(v.shape, v.dtype) for i, v in enumerate(small)]
    scratch += [
        *[pltpu.VMEM((n, pref, chunk, state), BF16)] * (2 * PARTS),
        *[pltpu.VMEM((n, piece, state), BF16)] * (4 * PARTS),
        *[pltpu.VMEM((slots + 1 + events, part, state), BF16)] * PARTS,
        *[pltpu.VMEM((part, state), BF16)] * PARTS,
        pltpu.VMEM((pref + 1, 32, 128), F32),
        pltpu.VMEM((pref + 1, 32, 128), BF16),
        pltpu.VMEM((n, pref, 16, 128), BF16),
        pltpu.VMEM((n, pref, 16, 128), BF16),
        pltpu.VMEM((events, 16, 128), BF16),
        pltpu.VMEM((events, 16, 128), BF16),
        pltpu.VMEM((n, 16, 128), BF16),
        pltpu.VMEM((n, 16, 128), BF16),
        pltpu.VMEM((events, 16, 128), BF16),
        pltpu.VMEM((events, 16, 128), BF16),
        pltpu.VMEM((32, 128), BF16),
        pltpu.VMEM((slots + 1 + events, tail, width + gw), F32),
        pltpu.VMEM((steps + tail, 8, width), F32),
        pltpu.VMEM((steps + tail, 8, gw), F32),
        pltpu.VMEM((steps, 8, width), F32),
        pltpu.VMEM((steps, 8, gw), F32),
        pltpu.VMEM((steps, 8, heads), F32),
        pltpu.VMEM((steps + 2, 8, heads), F32),
        pltpu.VMEM((steps, 8, width), F32),
        pltpu.VMEM((steps, 8, width), F32),
        pltpu.VMEM((steps, 8, width), F32),
        dma((3 * PARTS,)), dma((len(small),)),
        *[dma((2, PARTS))] * 7, dma((2, PARTS, 8)),
        *[dma((2,))] * 8,
        *[dma((PARTS + 1,))] * 2,
    ]
    shapes = (
        jax.ShapeDtypeStruct((steps, slots, width), BF16),
        jax.ShapeDtypeStruct(scan_state.shape, BF16),
        jax.ShapeDtypeStruct((slots, tail, width), BF16),
        jax.ShapeDtypeStruct((slots, tail, gw), BF16),
    )
    results = pl.pallas_call(
        functools.partial(kernel, n, PARTS, slots, pref, events, steps, heads, hsize, state),
        out_shape=shapes,
        in_specs=specs,
        out_specs=(vmem,) * 4,
        scratch_shapes=scratch,
        compiler_params=pltpu.CompilerParams(
            collective_id=0, has_side_effects=True, vmem_limit_bytes=40 * 1024 * 1024
        ),
    )(*args)
    layer, final_scan, final_inner, final_group = pl.pallas_call(
        finish,
        out_shape=shapes,
        in_specs=[hbm] * 4,
        out_specs=(hbm,) * 4,
        scratch_shapes=[dma((4,))],
        compiler_params=pltpu.CompilerParams(vmem_limit_bytes=40 * 1024 * 1024),
    )(*results)
    return layer.transpose(1, 0, 2), final_scan, final_inner, final_group.reshape(slots, tail, 1, gw)


def solution(mesh):
    count = mesh.shape["rep"]
    n = 1
    while n * n < count:
        n += 1
    placed = (
        P("rep", None, "ch"),
        P("rep", None, "ch", None),
        P("rep", None, "ch"),
        P("rep", None, "ch"),
        P("rep", "ch", None, None),
        P("rep", None, "ch"),
        P("rep", None, "ch", None),
        P("rep", "ch", None, None),
        P("rep", None, "ch"),
        P("rep", None, "ch", None),
        P(None, "ch"),
        P("ch"),
        P(None, "ch", None),
        P("ch", None),
        P("ch"),
        P("ch"),
        P("ch"),
        P("ch"),
        P(),
        P("rep"),
        P("rep"),
    )
    return jax.shard_map(
        functools.partial(on_device, n),
        mesh=mesh,
        in_specs=placed,
        out_specs=(
            P("rep", None, "ch"),
            P("rep", "ch", None, None),
            P("rep", None, "ch"),
            P("rep", None, "ch", None),
        ),
        check_vma=False,
    )
```

```python
import functools

import jax
import jax.numpy as jnp
from jax import lax
from jax.experimental import pallas as pl
from jax.experimental.pallas import tpu as pltpu
from jax.sharding import PartitionSpec as P

MESH = pl.DeviceIdType.MESH
BF16 = jnp.bfloat16
F32 = jnp.float32
EPSILON = 1e-05
PARTS = 1
MOVES = (((0, 0), (0, 1)), ((0, 2), (0, 3)), (), ())


def silu(v):
    return v / (1.0 + jnp.exp(-v))


def split2(v):
    high = v.astype(BF16)
    low = (v - high.astype(F32)).astype(BF16)
    return high, low


class Stream:
    def __init__(self, index, pos1, pos2, peer1, peer2, cand, red, cand2, candc, redc, candc2, conv):
        self.index = index
        self.pos1, self.pos2 = pos1, pos2
        self.peer1, self.peer2 = peer1, peer2
        self.cand, self.red, self.cand2 = cand, red, cand2
        self.candc, self.redc, self.candc2 = candc, redc, candc2
        self.conv = conv


def kernel(
    n, parts, slots, pref, events, steps, heads, hsize, state,
    *refs,
):
    inputs, refs = refs[:21], refs[21:]
    (out_ref, fin_ref, finner_ref, fgroup_ref), refs = refs[:4], refs[4:]
    held, refs = refs[:19], refs[19:]
    scan_hbm, pscan_hbm = inputs[4], inputs[7]
    (
        inner_ref, group_ref, gate_ref, dt_ref, cinner_ref, cgroup_ref, pinner_ref, pgroup_ref,
        ikern_ref, ibias_ref, gkern_ref, gbias_ref, decay_ref, dbias_ref, skip_ref, gain_ref, ep_ref, se_ref, mv_ref,
    ) = held
    blocks, refs = refs[: 8 * parts], refs[8 * parts :]
    cands, reds, cand2s = (blocks[2 * parts * i : 2 * parts * (i + 1)] for i in range(3))
    pools, stages = blocks[6 * parts : 7 * parts], blocks[7 * parts :]
    (
        pkf, pkb, candc_a, candc_b, redc_a, redc_b, candc2_a, candc2_b, conv_a, conv_b, camec, ucf,
        join, joing, xs, gs, dts, ms, us, ys, es, added,
        load_sem, small_sem, s1, r1, s2, r2, s3, r3, s4, r4, sc1, rc1, sc2, rc2, sc3, rc3, sc4, rc4, sm, rm,
    ) = refs
    rep = lax.axis_index("rep")
    total = n * n
    py = lax.rem(rep, n)
    pz = rep // n
    width = heads * hsize
    wrows = width // 128
    gw = 2 * state
    grows = gw // 128
    part = heads * hsize // parts
    share = part // 2
    chunk = share // n
    piece = events * chunk // n
    per_event = n // events
    base = slots + 1
    taps = ikern_ref.shape[0]
    tail = taps - 1

    def to(r):
        return {"rep": r}

    right = lax.rem(rep + 1, total)
    left = lax.rem(rep + total - 1, total)

    barrier = pltpu.get_barrier_semaphore()
    for d in (n // 2, *[x for k in range(n // 2 - 1, 0, -1) for x in (k, n - k)]):
        pl.semaphore_signal(barrier, inc=1, device_id=to(pz * n + lax.rem(py + d, n)), device_id_type=MESH)
        pl.semaphore_signal(barrier, inc=1, device_id=to(lax.rem(pz + d, n) * n + py), device_id_type=MESH)
    pl.semaphore_signal(barrier, inc=1, device_id=to(right), device_id_type=MESH)
    pl.semaphore_signal(barrier, inc=1, device_id=to(left), device_id_type=MESH)

    def chunk_rows(st, j):
        return pl.ds(pl.multiple_of(st * share + j * chunk, chunk), chunk)

    def all_rows(b, st, j):
        return pl.ds(pl.multiple_of(b * part + st * share + j * chunk, chunk), chunk)

    first = (6, 7, 4, 5, 18)
    rest = [v for i, v in enumerate(inputs) if i not in (4, 7)]
    small = [pltpu.make_async_copy(src, dst, small_sem.at[i]) for i, (src, dst) in enumerate(zip(rest, held))]
    for i in first:
        small[i].start()
    scan_loads = [
        pltpu.make_async_copy(
            scan_hbm.at[:, b * part : (b + 1) * part], pools[b].at[0:slots], load_sem.at[2 * parts + b]
        )
        for b in range(parts)
    ]
    for copy in scan_loads:
        copy.start()
    own_loads = {}
    for b in range(parts):
        for i, pos in enumerate((py, pz)):
            at = i * parts + b
            own_loads[i, b] = pltpu.make_async_copy(
                pscan_hbm.at[:, all_rows(b, i, pos)], cands[at].at[pos], load_sem.at[at]
            )
            own_loads[i, b].start()
    for i, copy in enumerate(small):
        if i not in first:
            copy.start()

    def copy_to(src, dst, send, recv, device):
        return pltpu.make_async_remote_copy(
            src_ref=src, dst_ref=dst, send_sem=send, recv_sem=recv, device_id=to(device), device_id_type=MESH
        )

    streams = (
        Stream(0, py, pz, lambda j: pz * n + j, lambda k: k * n + py,
               cands[:parts], reds[:parts], cand2s[:parts], candc_a, redc_a, candc2_a, conv_a),
        Stream(1, pz, py, lambda j: j * n + py, lambda k: pz * n + k,
               cands[parts:], reds[parts:], cand2s[parts:], candc_b, redc_b, candc2_b, conv_b),
    )

    def owner(st, e):
        rid = ep_ref[e]
        r = rid // pref
        y, z = lax.rem(r, n), r // n
        return (y, z, lax.rem(rid, pref)) if st.index == 0 else (z, y, lax.rem(rid, pref))

    def half(i):
        return slice(i * 16, (i + 1) * 16)

    def conv1_copy(st):
        return copy_to(
            pkb.at[0:pref, half(st.index)], st.candc.at[st.pos1], sc1.at[st.index], rc1.at[st.index], st.peer1(0)
        )

    def taken(ref, sem, way):
        copy = copy_to(ref, ref, sem, sem, right)
        copy.wait_send() if way == 0 else copy.wait_recv()

    def rs1_copy(st, b, d):
        j = lax.rem(st.pos1 + d, n)
        return copy_to(
            pscan_hbm.at[:, all_rows(b, st.index, j)], st.cand[b].at[st.pos1],
            s1.at[st.index, b], r1.at[st.index, b], st.peer1(j),
        )

    far_first = (n // 2, *[x for k in range(n // 2 - 1, 0, -1) for x in (k, n - k)])
    pl.semaphore_wait(barrier, 2 * (n - 1) + 2)

    def rs1_send(b):
        for d in far_first:
            for st in streams:
                rs1_copy(st, b, d).start()

    for b in range(parts):
        rs1_send(b)

    pkf[...] = jnp.zeros_like(pkf)
    for i in first:
        small[i].wait()
    moved = mv_ref[0]

    def pack(slot, inner_rows, group_rows):
        for tap in range(tail):
            for j in range(wrows):
                pkf[slot, tap * wrows + j : tap * wrows + j + 1, :] = inner_rows[tap][:, j * 128 : (j + 1) * 128]
            for j in range(grows):
                r = tail * wrows + tap * grows + j
                pkf[slot, r : r + 1, :] = group_rows[tap][:, j * 128 : (j + 1) * 128]

    p_inner = [pinner_ref[tap].astype(F32) for tap in range(tail)]
    p_group = [pgroup_ref[tap].astype(F32) for tap in range(tail)]
    for q in range(pref):
        pack(q, [v[q : q + 1] for v in p_inner], [v[q : q + 1] for v in p_group])
    m_inner = cinner_ref[moved].astype(F32)
    m_group = cgroup_ref[moved].astype(F32)
    pack(pref, [m_inner[t : t + 1] for t in range(tail)], [m_group[t : t + 1] for t in range(tail)])
    pkb[...] = pkf[...].astype(BF16)

    for st in streams:
        @pl.when(st.pos1 != 0)
        def _(st=st):
            conv1_copy(st).start()

    for b in range(parts):
        scan_loads[b].wait()
        for q in range(0, part, hsize):
            rows = slice(q, q + hsize)
            got = pools[b][0, rows]
            for s in range(1, slots):
                got = jnp.where(moved == s, pools[b][s, rows], got)
            stages[b][rows] = got
    conv_move = copy_to(pkb.at[pref], camec, sm.at[parts], rm.at[parts], right)
    conv_move.start()

    def move(b, i, count):
        rows = pl.ds(i * part // count, part // count)
        return copy_to(stages[b].at[rows], pools[b].at[slots, rows], sm.at[b], rm.at[b], right)

    for i, copy in enumerate(small):
        if i not in first:
            copy.wait()
    join[...] = jnp.zeros_like(join)
    joing[...] = jnp.zeros_like(joing)
    dts[...] = jnp.zeros_like(dts)
    for t in range(steps):
        join[tail + t, 0:slots, :] = inner_ref[t].astype(F32)
        joing[tail + t, 0:slots, :] = group_ref[t].astype(F32)
        if t >= steps - tail:
            for s in range(slots):
                k = t - (steps - tail)
                finner_ref[s, k : k + 1, :] = inner_ref[t, s : s + 1, :]
                fgroup_ref[s, k : k + 1, :] = group_ref[t, s : s + 1, :]
        dts[t, 0:slots, :] = dt_ref[t]
    for s in range(slots):
        ucf[s, :, 0:width] = cinner_ref[s].astype(F32)
        ucf[s, :, width : width + gw] = cgroup_ref[s].astype(F32)
    step = []
    decay = []
    for t in range(steps):
        v = dts[t] + dbias_ref[...]
        v = jnp.maximum(v, 0.0) + jnp.log1p(jnp.exp(-jnp.abs(v)))
        step.append(v)
        fall = -v * decay_ref[...]
        decay.append(fall if t == 0 else decay[-1] + fall)

    def conv2_copy(st, k):
        return copy_to(
            st.redc.at[k], st.candc2.at[st.pos2], sc2.at[st.index], rc2.at[st.index], st.peer2(k)
        )

    def conv_two(st):
        @pl.when(st.pos1 == 0)
        def _():
            taken(st.candc.at[1:n], rc1.at[st.index], 1)
            st.candc[0] = pkb[0:pref, half(st.index)]
            for e in range(events):
                p, _, row = owner(st, e)
                st.redc[e] = st.candc[p, row]
            for k in range(events):
                @pl.when(st.pos2 != k)
                def _(k=k):
                    conv2_copy(st, k).start()

                @pl.when(st.pos2 == k)
                def _(k=k):
                    st.candc2[k] = st.redc[k]

    def conv3_copy(st, d, e):
        k = lax.rem(st.pos2 + d, n)
        return copy_to(st.conv.at[e], st.conv.at[e], sc3.at[st.index], rc3.at[st.index], st.peer2(k))

    def conv_three(st):
        @pl.when(st.pos1 == 0)
        def _():
            for e in range(events):
                @pl.when(st.pos2 == e)
                def _(e=e):
                    taken(st.candc2.at[0 : n - 1], rc2.at[st.index], 1)
                    _, q, _ = owner(st, e)
                    st.conv[e] = st.candc2[q]
                    for d in range(1, n):
                        conv3_copy(st, d, e).start()

    def conv4_copy(st, d):
        j = lax.rem(st.pos1 + d, n)
        return copy_to(st.conv, st.conv, sc4.at[st.index], rc4.at[st.index], st.peer1(j))

    def conv_four(st):
        @pl.when(st.pos1 == 0)
        def _():
            @pl.when(st.pos2 < events)
            def _():
                taken(st.conv.at[0 : events - 1], rc3.at[st.index], 1)

            @pl.when(st.pos2 >= events)
            def _():
                taken(st.conv, rc3.at[st.index], 1)

            for d in range(1, n):
                conv4_copy(st, d).start()

    def conv_five(st):
        @pl.when(st.pos1 != 0)
        def _():
            taken(st.conv, rc4.at[st.index], 1)

    def rs2_copy(st, b, d):
        k = lax.rem(st.pos2 + d, n)
        return copy_to(
            st.red[b].at[k], st.cand2[b].at[st.pos2], s2.at[st.index, b], r2.at[st.index, b], st.peer2(k)
        )

    def rs_two(st, b):
        taken(st.cand[b].at[0 : n - 1], r1.at[st.index, b], 1)
        own_loads[st.index, b].wait()
        for e in range(events):
            p, _, row = owner(st, e)
            for u in range(per_event):
                st.red[b][e * per_event + u] = st.cand[b][p, row, u * piece : (u + 1) * piece, :]
        for d in far_first:
            rs2_copy(st, b, d).start()
        st.cand2[b][st.pos2] = st.red[b][st.pos2]

    def place(b, st, j, k):
        offset = pl.multiple_of(st.index * share + j * chunk + lax.rem(k, per_event) * piece, piece)
        return pools[b].at[base + k // per_event, pl.ds(offset, piece)]

    def ag1_copy(st, b, d):
        spot = place(b, st, st.pos1, st.pos2)
        return copy_to(spot, spot, s3.at[st.index, b], r3.at[st.index, b], st.peer2(lax.rem(st.pos2 + d, n)))

    def ag_one(st, b):
        taken(st.cand2[b].at[0 : n - 1], r2.at[st.index, b], 1)
        _, q, _ = owner(st, st.pos2 // per_event)
        place(b, st, st.pos1, st.pos2)[...] = st.cand2[b][q]
        for d in far_first:
            ag1_copy(st, b, d).start()

    pair = events // 2
    low, high, whole = (0, pair), (pair, events), (0, events)
    first_leg = [(0, 2) + low, (0, -2) + low, (0, 2) + high, (0, -2) + high, (0, 1) + whole, (0, -1) + whole]
    second_leg = [(-2, 2) + low, (-2, 1) + low, (2, -1) + low, (-2, 1) + high, (2, -2) + high, (2, -1) + high]
    handed = ((6, 7), (8,), (9,), (10, 11))
    if n == 4:
        first_leg = [(0, 2) + low, (0, -2) + high, (0, 1) + whole, (0, -1) + whole]
        second_leg = []
    legs = first_leg + second_leg

    def leg_spot(st, b, distance, first, last):
        j = lax.rem(st.pos1 + n + distance, n)
        return pools[b].at[base + first : base + last, chunk_rows(st.index, j)]

    def leg_send(st, b, some):
        for i in some:
            c, t, a, z = legs[i]
            spot = leg_spot(st, b, c, a, z)
            target = st.peer1(lax.rem(st.pos1 + n + t, n))
            copy_to(spot, spot, s4.at[st.index, b], r4.at[st.index, b, i], target).start()

    def leg_wait(st, b, some):
        for i in some:
            c, t, a, z = legs[i]
            taken(leg_spot(st, b, c - t, a, z), r4.at[st.index, b, i], 1)

    def spread(st, b):
        taken(st.cand2[b].at[0 : n - 1], r3.at[st.index, b], 1)
        leg_send(st, b, range(len(first_leg)))

    def hand_on(b):
        if second_leg:
            for i, some in enumerate(handed):
                for st in streams:
                    leg_wait(st, b, [i])
                    leg_send(st, b, some)

    def arrive(b):
        for st in streams:
            leg_wait(st, b, range(len(handed) if second_leg else 0, len(legs)))

    def each(phase, b):
        for st in streams:
            phase(st, b)

    def conv(phase):
        for st in streams:
            phase(st)

    def moves(when):
        for b, i in MOVES[when]:
            move(b, i, 4 // parts).start()

    for when, (phase, conv_phase) in enumerate(((rs_two, conv_two), (ag_one, conv_three), (spread, conv_four))):
        for b in range(parts):
            each(phase, b)
            if b == 0:
                conv(conv_phase)
        moves(when)
    for b in range(parts):
        hand_on(b)
    moves(3)
    conv(conv_five)
    conv_move.wait_recv()
    sources = [(base + e, e) for e in range(events)]

    def unpack(row, top, bottom):
        both = (top.astype(F32), bottom.astype(F32))
        for tap in range(tail):
            for j in range(wrows):
                r = tap * wrows + j
                ucf[row, tap : tap + 1, j * 128 : (j + 1) * 128] = both[r // 16][r % 16 : r % 16 + 1]
            for j in range(grows):
                r = tail * wrows + tap * grows + j
                ucf[row, tap : tap + 1, width + j * 128 : width + (j + 1) * 128] = both[r // 16][r % 16 : r % 16 + 1]

    for row, e in sources:
        unpack(row, conv_a[e], conv_b[e])
    unpack(slots, camec[0:16], camec[16:32])

    index = []
    for s in range(slots):
        e = se_ref[s]
        at = jnp.where(e >= 0, base + e, jnp.where(moved == s, slots, s))
        index.append(at)
        rows = ucf[at]
        for tap in range(tail):
            join[tap, s : s + 1, :] = rows[tap : tap + 1, 0:width]
            joing[tap, s : s + 1, :] = rows[tap : tap + 1, width : width + gw]


    for t in range(steps):
        v = ibias_ref[...].astype(F32).reshape(1, width)
        g = gbias_ref[...].astype(F32)
        for k in range(taps):
            v = v + ikern_ref[k : k + 1, :].astype(F32) * join[t + k]
            g = g + gkern_ref[k : k + 1, :].astype(F32) * joing[t + k]
        xs[t] = silu(v)
        gs[t] = silu(g)

    which = lax.broadcasted_iota(jnp.int32, (heads, width), 1) // hsize
    expand = (which == lax.broadcasted_iota(jnp.int32, (heads, width), 0)).astype(BF16)

    def widen(v):
        high, low = split2(v)
        return jnp.dot(high, expand, preferred_element_type=F32) + jnp.dot(low, expand, preferred_element_type=F32)

    for t in range(steps):
        c = gs[t, :, state:gw]
        for s in range(t + 1):
            dot = jnp.sum(c * gs[s, :, 0:state], axis=-1, keepdims=True)
            m = (step[s] if s == t else jnp.exp(decay[t] - decay[s]) * step[s]) * dot
            ms[s] = m + skip_ref[...] if s == t else m
        ms[t + 1] = jnp.exp(decay[t])
        ms[t + 2] = jnp.exp(decay[steps - 1] - decay[t]) * step[t]
        rows = ms[0 : t + 3].reshape(((t + 3) * 8, heads))
        wide = widen(rows).reshape((t + 3, 8, width))
        y = wide[0] * xs[0]
        for s in range(1, t + 1):
            y = y + wide[s] * xs[s]
        ys[t] = y
        es[t] = wide[t + 1]
        us[t] = wide[t + 2] * xs[t]

    eye = lax.broadcasted_iota(jnp.int32, (heads, heads), 0) == lax.broadcasted_iota(jnp.int32, (heads, heads), 1)
    last = jnp.exp(decay[steps - 1])
    diag = jnp.concatenate([jnp.where(eye, last[s : s + 1], 0.0) for s in range(slots)], axis=0)
    kept = jnp.dot(diag, jnp.ones((heads, state), F32), precision=lax.Precision.HIGHEST, preferred_element_type=F32)

    pad = jnp.zeros((16 - steps, state), F32)
    padw = jnp.zeros((16 - steps, width), F32)
    reads = []
    for s in range(slots):
        c_high, c_low = split2(jnp.concatenate([gs[:, s, state:gw], pad], axis=0))
        reads.append(jnp.concatenate([c_high, c_low], axis=0))
        b_high, b_low = split2(jnp.concatenate([gs[:, s, 0:state], pad], axis=0))
        u_high, u_low = split2(jnp.concatenate([us[:, s, :], padw], axis=0))
        added[s] = lax.dot_general(
            jnp.concatenate([u_high, u_low, u_high], axis=0),
            jnp.concatenate([b_high, b_high, b_low], axis=0),
            (((0,), (0,)), ((), ())), preferred_element_type=F32,
        )
    for t in range(steps):
        join[t, 0:slots, :] = silu(gate_ref[t].astype(F32))
    for b in range(parts):
        arrive(b)
        taken(stages[b], rm.at[b], 1)
        lanes = slice(b * part, (b + 1) * part)
        for s in range(slots):
            start = pools[b][index[s]]
            read = lax.dot_general(reads[s], start, (((1,), (1,)), ((), ())), preferred_element_type=F32)
            read = read[0:steps] + read[16 : 16 + steps]
            ys[:, s, lanes] = ys[:, s, lanes] + es[:, s, lanes] * read
            for q in range(part // hsize):
                rows = slice(q * hsize, (q + 1) * hsize)
                h = b * (part // hsize) + q
                k = s * heads + h
                fin_ref[s, h] = (kept[k : k + 1] * start[rows].astype(F32) + added[s, b * part + q * hsize : b * part + (q + 1) * hsize]).astype(BF16)

    for t in range(steps):
        y = ys[t, 0:slots, :] * join[t, 0:slots, :]
        mean = jnp.sum(y * y, axis=-1, keepdims=True) / width
        out_ref[t] = (y * lax.rsqrt(mean + EPSILON) * gain_ref[...]).astype(BF16)

    for st in streams:
        @pl.when(st.pos1 != 0)
        def _(st=st):
            conv1_copy(st).wait_send()

        @pl.when(st.pos1 == 0)
        def _(st=st):
            @pl.when(st.pos2 < events)
            def _():
                taken(st.conv.at[0 : events - 1], sc2.at[st.index], 0)
                taken(st.candc2.at[0 : n - 1], sc3.at[st.index], 0)

            @pl.when(st.pos2 >= events)
            def _():
                taken(st.conv, sc2.at[st.index], 0)

            taken(pools[0].at[base, 0 : (n - 1) * events * 16], sc4.at[st.index], 0)

        for b in range(parts):
            taken(st.cand[b].at[0 : n - 1], s1.at[st.index, b], 0)
            taken(st.red[b].at[0 : n - 1], s2.at[st.index, b], 0)
            taken(st.red[b].at[0 : n - 1], s3.at[st.index, b], 0)
            taken(pools[b].at[base : base + events, 0 : (n - 1) * chunk], s4.at[st.index, b], 0)
    conv_move.wait_send()
    for b in range(parts):
        taken(stages[b], sm.at[b], 0)


def finish(*refs):
    half = len(refs) // 2
    pairs = list(zip(refs[:half], refs[half:-1]))
    layer, scan, inner, group = pairs
    pairs = [(v.at[i], w.at[i]) for v, w in (scan,) for i in range(v.shape[0])]
    pairs += [layer, inner, group]
    copies = [pltpu.make_async_copy(v, w, refs[-1].at[i]) for i, (v, w) in enumerate(pairs)]
    for copy in copies:
        copy.start()
    for copy in copies:
        copy.wait()


def on_device(
    n,
    inner_input, group_input, gate_input, step_size, scan_state, conv_inner, conv_group,
    prefix_scan, prefix_inner, prefix_group, inner_kernel, inner_bias, group_kernel, group_bias,
    decay_rate, step_bias, skip_gain, norm_gain, event_prefix, slot_event, moved_slot,
):
    slots, steps, width = inner_input.shape
    pref, heads, hsize, state = prefix_scan.shape
    events = event_prefix.shape[0]
    taps = inner_kernel.shape[0]
    tail = taps - 1
    gw = group_input.shape[-1]
    part = heads * hsize // PARTS
    chunk = part // (2 * n)
    piece = events * chunk // n

    args = (
        inner_input.transpose(1, 0, 2),
        group_input.reshape(slots, steps, gw).transpose(1, 0, 2),
        gate_input.transpose(1, 0, 2),
        step_size.transpose(1, 0, 2),
        scan_state.reshape(slots, width, state),
        conv_inner,
        conv_group.reshape(slots, tail, gw),
        prefix_scan.reshape(pref, width, state),
        prefix_inner.transpose(1, 0, 2),
        prefix_group.reshape(pref, tail, gw).transpose(1, 0, 2),
        inner_kernel,
        inner_bias,
        group_kernel.reshape(taps, gw),
        group_bias.reshape(1, gw),
        decay_rate.reshape(1, heads),
        step_bias.reshape(1, heads),
        skip_gain.reshape(1, heads),
        norm_gain.reshape(1, width),
        event_prefix,
        slot_event,
        moved_slot,
    )
    vmem = pl.BlockSpec(memory_space=pltpu.VMEM)
    hbm = pl.BlockSpec(memory_space=pl.ANY)
    specs = [hbm] * len(args)
    small = [v for i, v in enumerate(args) if i not in (4, 7)]
    args = tuple(v if v.size == 1 else pltpu.with_memory_space_constraint(v, pltpu.HBM) for v in args)
    dma = pltpu.SemaphoreType.DMA
    scratch = [(pltpu.VMEM if i < len(small) - 3 else pltpu.SMEM)(v.shape, v.dtype) for i, v in enumerate(small)]
    scratch += [
        *[pltpu.VMEM((n, pref, chunk, state), BF16)] * (2 * PARTS),
        *[pltpu.VMEM((n, piece, state), BF16)] * (4 * PARTS),
        *[pltpu.VMEM((slots + 1 + events, part, state), BF16)] * PARTS,
        *[pltpu.VMEM((part, state), BF16)] * PARTS,
        pltpu.VMEM((pref + 1, 32, 128), F32),
        pltpu.VMEM((pref + 1, 32, 128), BF16),
        pltpu.VMEM((n, pref, 16, 128), BF16),
        pltpu.VMEM((n, pref, 16, 128), BF16),
        pltpu.VMEM((events, 16, 128), BF16),
        pltpu.VMEM((events, 16, 128), BF16),
        pltpu.VMEM((n, 16, 128), BF16),
        pltpu.VMEM((n, 16, 128), BF16),
        pltpu.VMEM((events, 16, 128), BF16),
        pltpu.VMEM((events, 16, 128), BF16),
        pltpu.VMEM((32, 128), BF16),
        pltpu.VMEM((slots + 1 + events, tail, width + gw), F32),
        pltpu.VMEM((steps + tail, 8, width), F32),
        pltpu.VMEM((steps + tail, 8, gw), F32),
        pltpu.VMEM((steps, 8, width), F32),
        pltpu.VMEM((steps, 8, gw), F32),
        pltpu.VMEM((steps, 8, heads), F32),
        pltpu.VMEM((steps + 2, 8, heads), F32),
        pltpu.VMEM((steps, 8, width), F32),
        pltpu.VMEM((steps, 8, width), F32),
        pltpu.VMEM((steps, 8, width), F32),
        pltpu.VMEM((slots, width, state), F32),
        dma((3 * PARTS,)), dma((len(small),)),
        *[dma((2, PARTS))] * 7, dma((2, PARTS, 12)),
        *[dma((2,))] * 8,
        *[dma((PARTS + 1,))] * 2,
    ]
    shapes = (
        jax.ShapeDtypeStruct((steps, slots, width), BF16),
        jax.ShapeDtypeStruct(scan_state.shape, BF16),
        jax.ShapeDtypeStruct((slots, tail, width), BF16),
        jax.ShapeDtypeStruct((slots, tail, gw), BF16),
    )
    results = pl.pallas_call(
        functools.partial(kernel, n, PARTS, slots, pref, events, steps, heads, hsize, state),
        out_shape=shapes,
        in_specs=specs,
        out_specs=(vmem,) * 4,
        scratch_shapes=scratch,
        compiler_params=pltpu.CompilerParams(
            collective_id=0, has_side_effects=True, vmem_limit_bytes=40 * 1024 * 1024
        ),
    )(*args)
    layer, final_scan, final_inner, final_group = pl.pallas_call(
        finish,
        out_shape=shapes,
        in_specs=[hbm] * 4,
        out_specs=(hbm,) * 4,
        scratch_shapes=[dma((slots + 3,))],
        compiler_params=pltpu.CompilerParams(vmem_limit_bytes=40 * 1024 * 1024),
    )(*results)
    return layer.transpose(1, 0, 2), final_scan, final_inner, final_group.reshape(slots, tail, 1, gw)


def solution(mesh):
    count = mesh.shape["rep"]
    n = 1
    while n * n < count:
        n += 1
    placed = (
        P("rep", None, "ch"),
        P("rep", None, "ch", None),
        P("rep", None, "ch"),
        P("rep", None, "ch"),
        P("rep", "ch", None, None),
        P("rep", None, "ch"),
        P("rep", None, "ch", None),
        P("rep", "ch", None, None),
        P("rep", None, "ch"),
        P("rep", None, "ch", None),
        P(None, "ch"),
        P("ch"),
        P(None, "ch", None),
        P("ch", None),
        P("ch"),
        P("ch"),
        P("ch"),
        P("ch"),
        P(),
        P("rep"),
        P("rep"),
    )
    return jax.shard_map(
        functools.partial(on_device, n),
        mesh=mesh,
        in_specs=placed,
        out_specs=(
            P("rep", None, "ch"),
            P("rep", "ch", None, None),
            P("rep", None, "ch"),
            P("rep", None, "ch", None),
        ),
        check_vma=False,
    )
```

```python
import functools

import jax
import jax.numpy as jnp
from jax import lax
from jax.experimental import pallas as pl
from jax.experimental.pallas import tpu as pltpu
from jax.sharding import PartitionSpec as P

MESH = pl.DeviceIdType.MESH
BF16 = jnp.bfloat16
F32 = jnp.float32
EPSILON = 1e-05
PARTS = 1
MOVES = (((0, 0), (0, 1)), ((1, 0), (1, 1)), (), ())


def silu(v):
    return v / (1.0 + jnp.exp(-v))


def split2(v):
    high = v.astype(BF16)
    low = (v - high.astype(F32)).astype(BF16)
    return high, low


class Stream:
    def __init__(self, index, pos1, pos2, peer1, peer2, cand, red, cand2, candc, redc, candc2, conv):
        self.index = index
        self.pos1, self.pos2 = pos1, pos2
        self.peer1, self.peer2 = peer1, peer2
        self.cand, self.red, self.cand2 = cand, red, cand2
        self.candc, self.redc, self.candc2 = candc, redc, candc2
        self.conv = conv


def kernel(
    n, parts, slots, pref, events, steps, heads, hsize, state,
    *refs,
):
    inputs, refs = refs[:21], refs[21:]
    (out_ref, fin_ref, finner_ref, fgroup_ref), refs = refs[:4], refs[4:]
    held, refs = refs[:19], refs[19:]
    scan_hbm, pscan_hbm = inputs[4], inputs[7]
    (
        inner_ref, group_ref, gate_ref, dt_ref, cinner_ref, cgroup_ref, pinner_ref, pgroup_ref,
        ikern_ref, ibias_ref, gkern_ref, gbias_ref, decay_ref, dbias_ref, skip_ref, gain_ref, ep_ref, se_ref, mv_ref,
    ) = held
    blocks, refs = refs[: 6 * parts + 4], refs[6 * parts + 4 :]
    cands, reds, cand2s = (blocks[2 * parts * i : 2 * parts * (i + 1)] for i in range(3))
    pools, stages = blocks[6 * parts : 6 * parts + 2], blocks[6 * parts + 2 :]
    (
        pkf, pkb, candc_a, candc_b, redc_a, redc_b, candc2_a, candc2_b, conv_a, conv_b, camec, ucf,
        join, joing, xs, gs, dts, ms, us, ys, es, added,
        load_sem, small_sem, s1, r1, s2, r2, s3, r3, s4, r4, sc1, rc1, sc2, rc2, sc3, rc3, sc4, rc4, sm, rm,
    ) = refs
    rep = lax.axis_index("rep")
    total = n * n
    py = lax.rem(rep, n)
    pz = rep // n
    width = heads * hsize
    wrows = width // 128
    gw = 2 * state
    grows = gw // 128
    part = heads * hsize // parts
    share = part // 2
    chunk = share // n
    piece = events * chunk // n
    per_event = n // events
    base = slots + 1
    taps = ikern_ref.shape[0]
    tail = taps - 1

    def to(r):
        return {"rep": r}

    right = lax.rem(rep + 1, total)
    left = lax.rem(rep + total - 1, total)

    barrier = pltpu.get_barrier_semaphore()
    for d in (n // 2, *[x for k in range(n // 2 - 1, 0, -1) for x in (k, n - k)]):
        pl.semaphore_signal(barrier, inc=1, device_id=to(pz * n + lax.rem(py + d, n)), device_id_type=MESH)
        pl.semaphore_signal(barrier, inc=1, device_id=to(lax.rem(pz + d, n) * n + py), device_id_type=MESH)
    pl.semaphore_signal(barrier, inc=1, device_id=to(right), device_id_type=MESH)
    pl.semaphore_signal(barrier, inc=1, device_id=to(left), device_id_type=MESH)

    def chunk_rows(st, j):
        return pl.ds(pl.multiple_of(st * share + j * chunk, chunk), chunk)

    def all_rows(b, st, j):
        return pl.ds(pl.multiple_of(b * part + st * share + j * chunk, chunk), chunk)

    first = (6, 7, 4, 5, 18)
    rest = [v for i, v in enumerate(inputs) if i not in (4, 7)]
    small = [pltpu.make_async_copy(src, dst, small_sem.at[i]) for i, (src, dst) in enumerate(zip(rest, held))]
    for i in first:
        small[i].start()
    scan_loads = [
        pltpu.make_async_copy(
            scan_hbm.at[:, b * share : (b + 1) * share], pools[b].at[0:slots], load_sem.at[2 * parts + b]
        )
        for b in range(2)
    ]
    for copy in scan_loads:
        copy.start()
    own_loads = {}
    for b in range(parts):
        for i, pos in enumerate((py, pz)):
            at = i * parts + b
            own_loads[i, b] = pltpu.make_async_copy(
                pscan_hbm.at[:, all_rows(b, i, pos)], cands[at].at[pos], load_sem.at[at]
            )
            own_loads[i, b].start()
    for i, copy in enumerate(small):
        if i not in first:
            copy.start()

    def copy_to(src, dst, send, recv, device):
        return pltpu.make_async_remote_copy(
            src_ref=src, dst_ref=dst, send_sem=send, recv_sem=recv, device_id=to(device), device_id_type=MESH
        )

    streams = (
        Stream(0, py, pz, lambda j: pz * n + j, lambda k: k * n + py,
               cands[:parts], reds[:parts], cand2s[:parts], candc_a, redc_a, candc2_a, conv_a),
        Stream(1, pz, py, lambda j: j * n + py, lambda k: pz * n + k,
               cands[parts:], reds[parts:], cand2s[parts:], candc_b, redc_b, candc2_b, conv_b),
    )

    def owner(st, e):
        rid = ep_ref[e]
        r = rid // pref
        y, z = lax.rem(r, n), r // n
        return (y, z, lax.rem(rid, pref)) if st.index == 0 else (z, y, lax.rem(rid, pref))

    def half(i):
        return slice(i * 16, (i + 1) * 16)

    def conv1_copy(st):
        return copy_to(
            pkb.at[0:pref, half(st.index)], st.candc.at[st.pos1], sc1.at[st.index], rc1.at[st.index], st.peer1(0)
        )

    def taken(ref, sem, way):
        copy = copy_to(ref, ref, sem, sem, right)
        copy.wait_send() if way == 0 else copy.wait_recv()

    def rs1_copy(st, b, d):
        j = lax.rem(st.pos1 + d, n)
        return copy_to(
            pscan_hbm.at[:, all_rows(b, st.index, j)], st.cand[b].at[st.pos1],
            s1.at[st.index, b], r1.at[st.index, b], st.peer1(j),
        )

    far_first = (n // 2, *[x for k in range(n // 2 - 1, 0, -1) for x in (k, n - k)])
    pl.semaphore_wait(barrier, 2 * (n - 1) + 2)

    def rs1_send(b):
        for d in far_first:
            for st in streams:
                rs1_copy(st, b, d).start()

    for b in range(parts):
        rs1_send(b)

    pkf[...] = jnp.zeros_like(pkf)
    for i in first:
        small[i].wait()
    moved = mv_ref[0]

    def pack(slot, inner_rows, group_rows):
        for tap in range(tail):
            for j in range(wrows):
                pkf[slot, tap * wrows + j : tap * wrows + j + 1, :] = inner_rows[tap][:, j * 128 : (j + 1) * 128]
            for j in range(grows):
                r = tail * wrows + tap * grows + j
                pkf[slot, r : r + 1, :] = group_rows[tap][:, j * 128 : (j + 1) * 128]

    p_inner = [pinner_ref[tap].astype(F32) for tap in range(tail)]
    p_group = [pgroup_ref[tap].astype(F32) for tap in range(tail)]
    for q in range(pref):
        pack(q, [v[q : q + 1] for v in p_inner], [v[q : q + 1] for v in p_group])
    m_inner = cinner_ref[moved].astype(F32)
    m_group = cgroup_ref[moved].astype(F32)
    pack(pref, [m_inner[t : t + 1] for t in range(tail)], [m_group[t : t + 1] for t in range(tail)])
    pkb[...] = pkf[...].astype(BF16)

    for st in streams:
        @pl.when(st.pos1 != 0)
        def _(st=st):
            conv1_copy(st).start()

    for b in range(2):
        scan_loads[b].wait()
        for q in range(0, share, hsize):
            rows = slice(q, q + hsize)
            got = pools[b][0, rows]
            for s in range(1, slots):
                got = jnp.where(moved == s, pools[b][s, rows], got)
            stages[b][rows] = got
    conv_move = copy_to(pkb.at[pref], camec, sm.at[2], rm.at[2], right)
    conv_move.start()

    def move(b, i, count):
        rows = pl.ds(i * share // count, share // count)
        return copy_to(stages[b].at[rows], pools[b].at[slots, rows], sm.at[b], rm.at[b], right)

    for i, copy in enumerate(small):
        if i not in first:
            copy.wait()
    join[...] = jnp.zeros_like(join)
    joing[...] = jnp.zeros_like(joing)
    dts[...] = jnp.zeros_like(dts)
    for t in range(steps):
        join[tail + t, 0:slots, :] = inner_ref[t].astype(F32)
        joing[tail + t, 0:slots, :] = group_ref[t].astype(F32)
        if t >= steps - tail:
            for s in range(slots):
                k = t - (steps - tail)
                finner_ref[s, k : k + 1, :] = inner_ref[t, s : s + 1, :]
                fgroup_ref[s, k : k + 1, :] = group_ref[t, s : s + 1, :]
        dts[t, 0:slots, :] = dt_ref[t]
    for s in range(slots):
        ucf[s, :, 0:width] = cinner_ref[s].astype(F32)
        ucf[s, :, width : width + gw] = cgroup_ref[s].astype(F32)
    step = []
    decay = []
    for t in range(steps):
        v = dts[t] + dbias_ref[...]
        v = jnp.maximum(v, 0.0) + jnp.log1p(jnp.exp(-jnp.abs(v)))
        step.append(v)
        fall = -v * decay_ref[...]
        decay.append(fall if t == 0 else decay[-1] + fall)

    def conv2_copy(st, k):
        return copy_to(
            st.redc.at[k], st.candc2.at[st.pos2], sc2.at[st.index], rc2.at[st.index], st.peer2(k)
        )

    def conv_two(st):
        @pl.when(st.pos1 == 0)
        def _():
            taken(st.candc.at[1:n], rc1.at[st.index], 1)
            st.candc[0] = pkb[0:pref, half(st.index)]
            for e in range(events):
                p, _, row = owner(st, e)
                st.redc[e] = st.candc[p, row]
            for k in range(events):
                @pl.when(st.pos2 != k)
                def _(k=k):
                    conv2_copy(st, k).start()

                @pl.when(st.pos2 == k)
                def _(k=k):
                    st.candc2[k] = st.redc[k]

    def conv3_copy(st, d, e):
        k = lax.rem(st.pos2 + d, n)
        return copy_to(st.conv.at[e], st.conv.at[e], sc3.at[st.index], rc3.at[st.index], st.peer2(k))

    def conv_three(st):
        @pl.when(st.pos1 == 0)
        def _():
            for e in range(events):
                @pl.when(st.pos2 == e)
                def _(e=e):
                    taken(st.candc2.at[0 : n - 1], rc2.at[st.index], 1)
                    _, q, _ = owner(st, e)
                    st.conv[e] = st.candc2[q]
                    for d in range(1, n):
                        conv3_copy(st, d, e).start()

    def conv4_copy(st, d):
        j = lax.rem(st.pos1 + d, n)
        return copy_to(st.conv, st.conv, sc4.at[st.index], rc4.at[st.index], st.peer1(j))

    def conv_four(st):
        @pl.when(st.pos1 == 0)
        def _():
            @pl.when(st.pos2 < events)
            def _():
                taken(st.conv.at[0 : events - 1], rc3.at[st.index], 1)

            @pl.when(st.pos2 >= events)
            def _():
                taken(st.conv, rc3.at[st.index], 1)

            for d in range(1, n):
                conv4_copy(st, d).start()

    def conv_five(st):
        @pl.when(st.pos1 != 0)
        def _():
            taken(st.conv, rc4.at[st.index], 1)

    def rs2_copy(st, b, d):
        k = lax.rem(st.pos2 + d, n)
        return copy_to(
            st.red[b].at[k], st.cand2[b].at[st.pos2], s2.at[st.index, b], r2.at[st.index, b], st.peer2(k)
        )

    def rs_two(st, b):
        taken(st.cand[b].at[0 : n - 1], r1.at[st.index, b], 1)
        own_loads[st.index, b].wait()
        for e in range(events):
            p, _, row = owner(st, e)
            for u in range(per_event):
                st.red[b][e * per_event + u] = st.cand[b][p, row, u * piece : (u + 1) * piece, :]
        for d in far_first:
            rs2_copy(st, b, d).start()
        st.cand2[b][st.pos2] = st.red[b][st.pos2]

    def place(b, st, j, k):
        offset = pl.multiple_of(j * chunk + lax.rem(k, per_event) * piece, piece)
        return pools[st.index].at[base + k // per_event, pl.ds(offset, piece)]

    def ag1_copy(st, b, d):
        spot = place(b, st, st.pos1, st.pos2)
        return copy_to(spot, spot, s3.at[st.index, b], r3.at[st.index, b], st.peer2(lax.rem(st.pos2 + d, n)))

    def ag_one(st, b):
        taken(st.cand2[b].at[0 : n - 1], r2.at[st.index, b], 1)
        _, q, _ = owner(st, st.pos2 // per_event)
        place(b, st, st.pos1, st.pos2)[...] = st.cand2[b][q]
        for d in far_first:
            ag1_copy(st, b, d).start()

    pair = events // 2
    low, high, whole = (0, pair), (pair, events), (0, events)
    first_leg = [(0, 2) + low, (0, -2) + low, (0, 2) + high, (0, -2) + high, (0, 1) + whole, (0, -1) + whole]
    second_leg = [(-2, 2) + low, (-2, 1) + low, (2, -1) + low, (-2, 1) + high, (2, -2) + high, (2, -1) + high]
    handed = ((6, 7), (8,), (9,), (10, 11))
    if n == 4:
        first_leg = [(0, 2) + low, (0, -2) + high, (0, 1) + whole, (0, -1) + whole]
        second_leg = []
    legs = first_leg + second_leg

    def leg_spot(st, b, distance, first, last):
        j = lax.rem(st.pos1 + n + distance, n)
        return pools[st.index].at[base + first : base + last, chunk_rows(0, j)]

    def leg_send(st, b, some):
        for i in some:
            c, t, a, z = legs[i]
            spot = leg_spot(st, b, c, a, z)
            target = st.peer1(lax.rem(st.pos1 + n + t, n))
            copy_to(spot, spot, s4.at[st.index, b], r4.at[st.index, b, i], target).start()

    def leg_wait(st, b, some):
        for i in some:
            c, t, a, z = legs[i]
            taken(leg_spot(st, b, c - t, a, z), r4.at[st.index, b, i], 1)

    def spread(st, b):
        taken(st.cand2[b].at[0 : n - 1], r3.at[st.index, b], 1)
        leg_send(st, b, range(len(first_leg)))

    def hand_on(b):
        if second_leg:
            for i, some in enumerate(handed):
                for st in streams:
                    leg_wait(st, b, [i])
                    leg_send(st, b, some)

    def arrive(st):
        for b in range(parts):
            leg_wait(st, b, range(len(handed) if second_leg else 0, len(legs)))

    def each(phase, b):
        for st in streams:
            phase(st, b)

    def conv(phase):
        for st in streams:
            phase(st)

    def moves(when):
        for b, i in MOVES[when]:
            move(b, i, 2).start()

    for when, (phase, conv_phase) in enumerate(((rs_two, conv_two), (ag_one, conv_three), (spread, conv_four))):
        for b in range(parts):
            each(phase, b)
            if b == 0:
                conv(conv_phase)
        moves(when)
    for b in range(parts):
        hand_on(b)
    moves(3)
    conv(conv_five)
    conv_move.wait_recv()
    sources = [(base + e, e) for e in range(events)]

    def unpack(row, top, bottom):
        both = (top.astype(F32), bottom.astype(F32))
        for tap in range(tail):
            for j in range(wrows):
                r = tap * wrows + j
                ucf[row, tap : tap + 1, j * 128 : (j + 1) * 128] = both[r // 16][r % 16 : r % 16 + 1]
            for j in range(grows):
                r = tail * wrows + tap * grows + j
                ucf[row, tap : tap + 1, width + j * 128 : width + (j + 1) * 128] = both[r // 16][r % 16 : r % 16 + 1]

    for row, e in sources:
        unpack(row, conv_a[e], conv_b[e])
    unpack(slots, camec[0:16], camec[16:32])

    index = []
    for s in range(slots):
        e = se_ref[s]
        at = jnp.where(e >= 0, base + e, jnp.where(moved == s, slots, s))
        index.append(at)
        rows = ucf[at]
        for tap in range(tail):
            join[tap, s : s + 1, :] = rows[tap : tap + 1, 0:width]
            joing[tap, s : s + 1, :] = rows[tap : tap + 1, width : width + gw]


    for t in range(steps):
        v = ibias_ref[...].astype(F32).reshape(1, width)
        g = gbias_ref[...].astype(F32)
        for k in range(taps):
            v = v + ikern_ref[k : k + 1, :].astype(F32) * join[t + k]
            g = g + gkern_ref[k : k + 1, :].astype(F32) * joing[t + k]
        xs[t] = silu(v)
        gs[t] = silu(g)

    which = lax.broadcasted_iota(jnp.int32, (heads, width), 1) // hsize
    expand = (which == lax.broadcasted_iota(jnp.int32, (heads, width), 0)).astype(BF16)

    def widen(v):
        high, low = split2(v)
        return jnp.dot(high, expand, preferred_element_type=F32) + jnp.dot(low, expand, preferred_element_type=F32)

    for t in range(steps):
        c = gs[t, :, state:gw]
        for s in range(t + 1):
            dot = jnp.sum(c * gs[s, :, 0:state], axis=-1, keepdims=True)
            m = (step[s] if s == t else jnp.exp(decay[t] - decay[s]) * step[s]) * dot
            ms[s] = m + skip_ref[...] if s == t else m
        ms[t + 1] = jnp.exp(decay[t])
        ms[t + 2] = jnp.exp(decay[steps - 1] - decay[t]) * step[t]
        rows = ms[0 : t + 3].reshape(((t + 3) * 8, heads))
        wide = widen(rows).reshape((t + 3, 8, width))
        y = wide[0] * xs[0]
        for s in range(1, t + 1):
            y = y + wide[s] * xs[s]
        ys[t] = y
        es[t] = wide[t + 1]
        us[t] = wide[t + 2] * xs[t]

    eye = lax.broadcasted_iota(jnp.int32, (heads, heads), 0) == lax.broadcasted_iota(jnp.int32, (heads, heads), 1)
    last = jnp.exp(decay[steps - 1])
    diag = jnp.concatenate([jnp.where(eye, last[s : s + 1], 0.0) for s in range(slots)], axis=0)
    kept = jnp.dot(diag, jnp.ones((heads, state), F32), precision=lax.Precision.HIGHEST, preferred_element_type=F32)

    pad = jnp.zeros((16 - steps, state), F32)
    padw = jnp.zeros((16 - steps, width), F32)
    reads = []
    for s in range(slots):
        c_high, c_low = split2(jnp.concatenate([gs[:, s, state:gw], pad], axis=0))
        reads.append(jnp.concatenate([c_high, c_low], axis=0))
        b_high, b_low = split2(jnp.concatenate([gs[:, s, 0:state], pad], axis=0))
        u_high, u_low = split2(jnp.concatenate([us[:, s, :], padw], axis=0))
        added[s] = lax.dot_general(
            jnp.concatenate([u_high, u_low, u_high], axis=0),
            jnp.concatenate([b_high, b_high, b_low], axis=0),
            (((0,), (0,)), ((), ())), preferred_element_type=F32,
        )
    for t in range(steps):
        join[t, 0:slots, :] = silu(gate_ref[t].astype(F32))
    for b in range(2):
        arrive(streams[b])
        taken(stages[b], rm.at[b], 1)
        lanes = slice(b * share, (b + 1) * share)
        for s in range(slots):
            start = pools[b][index[s]]
            read = lax.dot_general(reads[s], start, (((1,), (1,)), ((), ())), preferred_element_type=F32)
            read = read[0:steps] + read[16 : 16 + steps]
            ys[:, s, lanes] = ys[:, s, lanes] + es[:, s, lanes] * read
            for q in range(share // hsize):
                rows = slice(q * hsize, (q + 1) * hsize)
                h = b * (share // hsize) + q
                k = s * heads + h
                fin_ref[s, h] = (kept[k : k + 1] * start[rows].astype(F32) + added[s, b * share + q * hsize : b * share + (q + 1) * hsize]).astype(BF16)

    for t in range(steps):
        y = ys[t, 0:slots, :] * join[t, 0:slots, :]
        mean = jnp.sum(y * y, axis=-1, keepdims=True) / width
        out_ref[t] = (y * lax.rsqrt(mean + EPSILON) * gain_ref[...]).astype(BF16)

    for st in streams:
        @pl.when(st.pos1 != 0)
        def _(st=st):
            conv1_copy(st).wait_send()

        @pl.when(st.pos1 == 0)
        def _(st=st):
            @pl.when(st.pos2 < events)
            def _():
                taken(st.conv.at[0 : events - 1], sc2.at[st.index], 0)
                taken(st.candc2.at[0 : n - 1], sc3.at[st.index], 0)

            @pl.when(st.pos2 >= events)
            def _():
                taken(st.conv, sc2.at[st.index], 0)

            taken(pools[0].at[base, 0 : (n - 1) * events * 16], sc4.at[st.index], 0)

        for b in range(parts):
            taken(st.cand[b].at[0 : n - 1], s1.at[st.index, b], 0)
            taken(st.red[b].at[0 : n - 1], s2.at[st.index, b], 0)
            taken(st.red[b].at[0 : n - 1], s3.at[st.index, b], 0)
            taken(pools[st.index].at[base : base + events, 0 : (n - 1) * chunk], s4.at[st.index, b], 0)
    conv_move.wait_send()
    for b in range(2):
        taken(stages[b], sm.at[b], 0)


def finish(*refs):
    half = len(refs) // 2
    pairs = list(zip(refs[:half], refs[half:-1]))
    layer, scan, inner, group = pairs
    pairs = [(v.at[i], w.at[i]) for v, w in (scan,) for i in range(v.shape[0])]
    pairs += [layer, inner, group]
    copies = [pltpu.make_async_copy(v, w, refs[-1].at[i]) for i, (v, w) in enumerate(pairs)]
    for copy in copies:
        copy.start()
    for copy in copies:
        copy.wait()


def on_device(
    n,
    inner_input, group_input, gate_input, step_size, scan_state, conv_inner, conv_group,
    prefix_scan, prefix_inner, prefix_group, inner_kernel, inner_bias, group_kernel, group_bias,
    decay_rate, step_bias, skip_gain, norm_gain, event_prefix, slot_event, moved_slot,
):
    slots, steps, width = inner_input.shape
    pref, heads, hsize, state = prefix_scan.shape
    events = event_prefix.shape[0]
    taps = inner_kernel.shape[0]
    tail = taps - 1
    gw = group_input.shape[-1]
    part = heads * hsize // PARTS
    chunk = part // (2 * n)
    piece = events * chunk // n

    args = (
        inner_input.transpose(1, 0, 2),
        group_input.reshape(slots, steps, gw).transpose(1, 0, 2),
        gate_input.transpose(1, 0, 2),
        step_size.transpose(1, 0, 2),
        scan_state.reshape(slots, width, state),
        conv_inner,
        conv_group.reshape(slots, tail, gw),
        prefix_scan.reshape(pref, width, state),
        prefix_inner.transpose(1, 0, 2),
        prefix_group.reshape(pref, tail, gw).transpose(1, 0, 2),
        inner_kernel,
        inner_bias,
        group_kernel.reshape(taps, gw),
        group_bias.reshape(1, gw),
        decay_rate.reshape(1, heads),
        step_bias.reshape(1, heads),
        skip_gain.reshape(1, heads),
        norm_gain.reshape(1, width),
        event_prefix,
        slot_event,
        moved_slot,
    )
    vmem = pl.BlockSpec(memory_space=pltpu.VMEM)
    hbm = pl.BlockSpec(memory_space=pl.ANY)
    specs = [hbm] * len(args)
    small = [v for i, v in enumerate(args) if i not in (4, 7)]
    args = tuple(v if v.size == 1 else pltpu.with_memory_space_constraint(v, pltpu.HBM) for v in args)
    dma = pltpu.SemaphoreType.DMA
    scratch = [(pltpu.VMEM if i < len(small) - 3 else pltpu.SMEM)(v.shape, v.dtype) for i, v in enumerate(small)]
    scratch += [
        *[pltpu.VMEM((n, pref, chunk, state), BF16)] * (2 * PARTS),
        *[pltpu.VMEM((n, piece, state), BF16)] * (4 * PARTS),
        *[pltpu.VMEM((slots + 1 + events, part // 2, state), BF16)] * 2,
        *[pltpu.VMEM((part // 2, state), BF16)] * 2,
        pltpu.VMEM((pref + 1, 32, 128), F32),
        pltpu.VMEM((pref + 1, 32, 128), BF16),
        pltpu.VMEM((n, pref, 16, 128), BF16),
        pltpu.VMEM((n, pref, 16, 128), BF16),
        pltpu.VMEM((events, 16, 128), BF16),
        pltpu.VMEM((events, 16, 128), BF16),
        pltpu.VMEM((n, 16, 128), BF16),
        pltpu.VMEM((n, 16, 128), BF16),
        pltpu.VMEM((events, 16, 128), BF16),
        pltpu.VMEM((events, 16, 128), BF16),
        pltpu.VMEM((32, 128), BF16),
        pltpu.VMEM((slots + 1 + events, tail, width + gw), F32),
        pltpu.VMEM((steps + tail, 8, width), F32),
        pltpu.VMEM((steps + tail, 8, gw), F32),
        pltpu.VMEM((steps, 8, width), F32),
        pltpu.VMEM((steps, 8, gw), F32),
        pltpu.VMEM((steps, 8, heads), F32),
        pltpu.VMEM((steps + 2, 8, heads), F32),
        pltpu.VMEM((steps, 8, width), F32),
        pltpu.VMEM((steps, 8, width), F32),
        pltpu.VMEM((steps, 8, width), F32),
        pltpu.VMEM((slots, width, state), F32),
        dma((2 * PARTS + 2,)), dma((len(small),)),
        *[dma((2, PARTS))] * 7, dma((2, PARTS, 12)),
        *[dma((2,))] * 8,
        *[dma((3,))] * 2,
    ]
    shapes = (
        jax.ShapeDtypeStruct((steps, slots, width), BF16),
        jax.ShapeDtypeStruct(scan_state.shape, BF16),
        jax.ShapeDtypeStruct((slots, tail, width), BF16),
        jax.ShapeDtypeStruct((slots, tail, gw), BF16),
    )
    results = pl.pallas_call(
        functools.partial(kernel, n, PARTS, slots, pref, events, steps, heads, hsize, state),
        out_shape=shapes,
        in_specs=specs,
        out_specs=(vmem,) * 4,
        scratch_shapes=scratch,
        compiler_params=pltpu.CompilerParams(
            collective_id=0, has_side_effects=True, vmem_limit_bytes=40 * 1024 * 1024
        ),
    )(*args)
    layer, final_scan, final_inner, final_group = pl.pallas_call(
        finish,
        out_shape=shapes,
        in_specs=[hbm] * 4,
        out_specs=(hbm,) * 4,
        scratch_shapes=[dma((slots + 3,))],
        compiler_params=pltpu.CompilerParams(vmem_limit_bytes=40 * 1024 * 1024),
    )(*results)
    return layer.transpose(1, 0, 2), final_scan, final_inner, final_group.reshape(slots, tail, 1, gw)


def solution(mesh):
    count = mesh.shape["rep"]
    n = 1
    while n * n < count:
        n += 1
    placed = (
        P("rep", None, "ch"),
        P("rep", None, "ch", None),
        P("rep", None, "ch"),
        P("rep", None, "ch"),
        P("rep", "ch", None, None),
        P("rep", None, "ch"),
        P("rep", None, "ch", None),
        P("rep", "ch", None, None),
        P("rep", None, "ch"),
        P("rep", None, "ch", None),
        P(None, "ch"),
        P("ch"),
        P(None, "ch", None),
        P("ch", None),
        P("ch"),
        P("ch"),
        P("ch"),
        P("ch"),
        P(),
        P("rep"),
        P("rep"),
    )
    return jax.shard_map(
        functools.partial(on_device, n),
        mesh=mesh,
        in_specs=placed,
        out_specs=(
            P("rep", None, "ch"),
            P("rep", "ch", None, None),
            P("rep", None, "ch"),
            P("rep", None, "ch", None),
        ),
        check_vma=False,
    )
```
